256 devices in a mesh: grp: 8 (over z_lo, x), sub: 32 (over z_hi, y, core).
Axes of the slice: x: 4, y: 4, z: 8 (z_hi: 4, z_lo: 2; z = z_hi * 2 + z_lo), core: 2. Of those that a mesh axis runs over, the one named last changes fastest.
Arguments:
- load_cases: float32 [294912, 128], P(('grp', 'sub')), may hold values from -6 to 6
- schur_matrix: float32 [294912, 1152], P(('grp', 'sub')), may hold values from -0.0017361111 to 16, as said below
- local_inverse: float32 [294912, 1152], P(('grp', 'sub')), may hold values from -0.00021701389 to 2, as said below
- coarse_basis: float32 [8192, 1152], P(('grp', 'sub')), may hold values from -0.375 to 0.375
- group_inverse: float32 [8192, 1024], P(('grp', 'sub')), may hold values from -0.00048828125 to 4, as said below
- group_modes: float32 [8192, 32], P(('grp', 'sub')), may hold values from -0.375 to 0.375
- top_inverse: float32 [256, 256], replicated, may hold values from -0.001953125 to 4, as said below
- face_map: int32 [256, 1152], P(('grp', 'sub')), may hold values from 0 to 1151, each once within a row
- spectrum: float32 [2], replicated, may hold values from 0.1 to 6, as said below
Outputs:
- solution: float32 [294912, 128], P(('grp', 'sub'))
- residual: float32 [294912, 128], P(('grp', 'sub'))
The draws below stay inside these ranges and needn't reach their ends.
Inputs may be any that keep to these rules, and one draw needn't show every extreme that they name: `face_map`: each row is a permutation of 0 to 1151. `schur_matrix`: each subdomain's 1152 x 1152 block is symmetric positive definite. `local_inverse`: each subdomain's 1152 x 1152 block is symmetric positive definite. `group_inverse`: each group's 1024 x 1024 block is symmetric positive definite. `top_inverse`: symmetric positive definite. spectrum[0] < spectrum[1].
All inputs are finite; a program needn't handle non-finite values.
Results may differ from the reference program's by a relative error of at most 0.00011.
Values sent between devices are 32-bit elements; how exact they have to be, the bound alone decides.
No kernel may reach another device: no remote copies, remote signals or barrier semaphores. Data moves between devices by JAX's collectives and lax.ppermute only.
A program may use at most 64 MiB of HBM per device.

```python
import math
import jax
import jax.numpy as jnp
from jax import lax

FACE = 288
ORDER = 1152
MODES = 32
CASES = 128
ITERS = 3
DOMAINS = 256
COARSE = 1024
APEX_DOFS = 256
N_GRP = 8
N_SUB = 32


def dominant(key, number, order, spread, diag_low, diag_high):
    first_key, second_key = jax.random.split(key)
    raw = jax.random.uniform(first_key, (number, order, order), jnp.float32, -1.0, 1.0)
    offdiag = (raw + jnp.swapaxes(raw, 1, 2)) * (0.5 * spread / order)
    levels = jnp.exp(jax.random.uniform(second_key, (number, order, 1), jnp.float32, math.log(diag_low), math.log(diag_high)))
    diagonal_mask = lax.broadcasted_iota(jnp.int32, (order, order), 0) == lax.broadcasted_iota(jnp.int32, (order, order), 1)
    return jnp.where(diagonal_mask[None], levels, offdiag)


def draw_schur_matrix(key, part):
    blocks = dominant(key, DOMAINS, ORDER, 2.0, 2.0, 4.0)
    return blocks.reshape(DOMAINS * ORDER, ORDER)


def draw_local_inverse(key, part):
    blocks = dominant(key, DOMAINS, ORDER, 0.25, 0.25, 0.5)
    return blocks.reshape(DOMAINS * ORDER, ORDER)


def draw_group_inverse(key, part):
    groups = APEX_DOFS // MODES
    blocks = dominant(key, groups, COARSE, 0.5, 0.5, 1.0)
    return blocks.reshape(groups * COARSE, COARSE)


def draw_top_inverse(key, part):
    blocks = dominant(key, 1, APEX_DOFS, 0.5, 0.5, 1.0)
    return blocks[0]


def draw_spectrum(key, part):
    first_key, second_key = jax.random.split(key)
    lower = jax.random.uniform(first_key, (), jnp.float32, 0.2, 0.4)
    upper = jax.random.uniform(second_key, (), jnp.float32, 2.5, 4.0)
    return jnp.stack([lower, upper])


def shard_levels(stream_key, shape, cuts, low, top_value):
    loudness, own = 1.0, jax.random.fold_in(stream_key, 6)
    for dim, parts in cuts:
        draws = jnp.exp(jax.random.uniform(jax.random.fold_in(own, dim), (parts,), jnp.float32, low / len(cuts), top_value / len(cuts)))
        loudness = loudness * jnp.repeat(draws, shape[dim] // parts).reshape([-1 if axis == dim else 1 for axis in range(len(shape))])
    return loudness


def normal_values(rng, dims, deviation, limit, shards=(), held_as=jnp.bfloat16):
    level = shard_levels(rng, dims, shards, -0.22, 0.18) if shards else 1.0
    values = jax.random.normal(rng, dims, jnp.float32) * deviation * level
    return jnp.minimum(jnp.maximum(values, -limit), limit).astype(held_as)


def setup_inputs(seed: int = 0) -> dict:
    key_of = jax.random.split(jax.random.key(seed), 10)
    load_cases = normal_values(key_of[0], (DOMAINS * ORDER, CASES), 1.0, 6.0, ((0, 256),), jnp.float32)
    schur_matrix = draw_schur_matrix(jax.random.fold_in(key_of[9], 71), 0)
    local_inverse = draw_local_inverse(jax.random.fold_in(key_of[9], 71), 0)
    coarse_basis = normal_values(key_of[3], (DOMAINS * MODES, ORDER), (ORDER // 4) ** -0.5, 0.375, ((0, 256),), jnp.float32)
    group_inverse = draw_group_inverse(jax.random.fold_in(key_of[9], 71), 0)
    group_modes = normal_values(key_of[5], (DOMAINS * MODES, MODES), (8 * MODES) ** -0.5, 0.375, ((0, 256),), jnp.float32)
    top_inverse = draw_top_inverse(jax.random.fold_in(key_of[9], 71), 0)
    face_map = jax.vmap(lambda own: jax.random.permutation(own, ORDER))(jax.random.split(key_of[7], DOMAINS)).reshape((DOMAINS, ORDER)).astype(jnp.int32)
    spectrum = draw_spectrum(jax.random.fold_in(key_of[9], 71), 0)
    return dict(load_cases=load_cases, schur_matrix=schur_matrix, local_inverse=local_inverse, coarse_basis=coarse_basis, group_inverse=group_inverse, group_modes=group_modes, top_inverse=top_inverse, face_map=face_map, spectrum=spectrum)


def assemble(values, face_map, inverse_map):
    columns = values.shape[-1]
    face_rows = jnp.take_along_axis(values, face_map[:, :, None], axis=1).reshape(N_GRP, N_SUB, 4, FACE, columns)
    zero_grp = jnp.zeros_like(face_rows[:1, :, 0])
    zero_sub = jnp.zeros_like(face_rows[:, :1, 0])
    from_low = jnp.concatenate([zero_grp, face_rows[:-1, :, 1]], axis=0)
    from_high = jnp.concatenate([face_rows[1:, :, 0], zero_grp], axis=0)
    from_left = jnp.concatenate([zero_sub, face_rows[:, :-1, 3]], axis=1)
    from_right = jnp.concatenate([face_rows[:, 1:, 2], zero_sub], axis=1)
    received = jnp.stack([from_low, from_high, from_left, from_right], axis=2).reshape(DOMAINS, ORDER, columns)
    return values + jnp.take_along_axis(received, inverse_map[:, :, None], axis=1)


def reference(load_cases, schur_matrix, local_inverse, coarse_basis, group_inverse, group_modes, top_inverse, face_map, spectrum):
    largest_bound = lax.Precision.HIGHEST
    inverse_map = jnp.argsort(face_map, axis=1).astype(jnp.int32)
    grp_ids = jnp.arange(N_GRP)[:, None]
    sub_ids = jnp.arange(N_SUB)[None, :]
    has_side = jnp.stack([jnp.broadcast_to(grp_ids > 0, (N_GRP, N_SUB)),
                          jnp.broadcast_to(grp_ids < N_GRP - 1, (N_GRP, N_SUB)),
                          jnp.broadcast_to(sub_ids > 0, (N_GRP, N_SUB)),
                          jnp.broadcast_to(sub_ids < N_SUB - 1, (N_GRP, N_SUB))], axis=-1)
    face_weight = jnp.where(has_side, 0.5, 1.0).astype(jnp.float32).reshape(DOMAINS, 4)
    face_weight = jnp.repeat(face_weight, FACE, axis=1)
    weight = jnp.take_along_axis(face_weight, inverse_map, axis=1)[:, :, None]

    schur_blocks = schur_matrix.reshape(DOMAINS, ORDER, ORDER)
    inverse_blocks = local_inverse.reshape(DOMAINS, ORDER, ORDER)
    basis = coarse_basis.reshape(DOMAINS, MODES, ORDER)
    group_blocks = group_inverse.reshape(N_GRP, COARSE, COARSE)
    cluster_basis = group_modes.reshape(N_GRP, COARSE, MODES)

    def precondition(residual):
        weighted = weight * residual
        local_part = jnp.einsum('dab,dbr->dar', inverse_blocks, weighted, precision=largest_bound)
        coarse = jnp.einsum('dma,dar->dmr', basis, weighted, precision=largest_bound)
        piled_vectors = coarse.reshape(N_GRP, COARSE, -1)
        cluster_portion = jnp.einsum('gab,gbr->gar', group_blocks, piled_vectors, precision=largest_bound)
        apex_input = jnp.einsum('kli,klp->kip', cluster_basis, piled_vectors, precision=largest_bound).reshape(APEX_DOFS, -1)
        apex_output = jnp.dot(top_inverse, apex_input, precision=largest_bound).reshape(N_GRP, MODES, -1)
        update_term = cluster_portion + jnp.einsum('usl,ule->use', cluster_basis, apex_output, precision=largest_bound)
        update_term = update_term.reshape(DOMAINS, MODES, -1)
        summed = local_part + jnp.einsum('dma,dmr->dar', basis, update_term, precision=largest_bound)
        return assemble(weight * summed, face_map, inverse_map)

    centre = 0.5 * (spectrum[0] + spectrum[1])
    half_width = 0.5 * (spectrum[1] - spectrum[0])
    residual = assemble(load_cases.reshape(DOMAINS, ORDER, CASES), face_map, inverse_map)
    direction = precondition(residual) / centre
    rho_now = half_width / centre
    solution = jnp.zeros_like(residual)
    for turn_index in range(ITERS):
        solution = solution + direction
        applied = jnp.einsum('dab,dbr->dar', schur_blocks, direction, precision=largest_bound)
        residual = residual - assemble(applied, face_map, inverse_map)
        if turn_index + 1 < ITERS:
            rho_next = 1.0 / (2.0 * centre / half_width - rho_now)
            direction = rho_next * rho_now * direction + (2.0 * rho_next / half_width) * precondition(residual)
            rho_now = rho_next
    return solution.reshape(DOMAINS * ORDER, CASES), residual.reshape(DOMAINS * ORDER, CASES)
```

```python
import functools

import jax
import jax.numpy as jnp
from jax import lax
from jax.experimental import pallas as pl
from jax.experimental.pallas import tpu as pltpu
from jax.sharding import PartitionSpec as P

ITERS = 3
F32, BF16 = jnp.float32, jnp.bfloat16
EXACT = lax.Precision.HIGHEST
VMEM = pl.BlockSpec(memory_space=pltpu.VMEM)
SMEM = pl.BlockSpec(memory_space=pltpu.SMEM)


def call(kernel, outs, ins, scratch=(), limit=24 << 20, flops=1 << 20):
    specs = [SMEM if kind == "s" else VMEM for kind, _ in ins]
    results = pl.pallas_call(
        kernel,
        out_shape=[jax.ShapeDtypeStruct(shape, dtype) for shape, dtype in outs],
        in_specs=specs,
        out_specs=[VMEM] * len(outs),
        scratch_shapes=list(scratch),
        compiler_params=pltpu.CompilerParams(vmem_limit_bytes=limit),
        cost_estimate=pl.CostEstimate(flops=flops, bytes_accessed=1 << 20, transcendentals=0),
    )(*[array for _, array in ins])
    return list(results)


def halves(x):
    high = x.astype(BF16)
    return high, (x - high.astype(F32)).astype(BF16)


def paired(x):
    return jnp.concatenate(halves(x), axis=1)


def dot(a, b):
    return jnp.dot(a, b, preferred_element_type=F32)


def dot_first(a, b):
    return lax.dot_general(a, b, (((0,), (0,)), ((), ())), preferred_element_type=F32)


def folded(x):
    columns = x.shape[1] // 2
    return x[:, :columns] + x[:, columns:]


def reorder(onehot, x):
    return folded(dot(onehot, paired(x)))


def reorder_whole(onehot, x):
    columns = x.shape[1]
    high, low = halves(x)
    rest = (x - high.astype(F32) - low.astype(F32)).astype(BF16)
    moved = dot(onehot, jnp.concatenate([high, low, rest], axis=1))
    return moved[:, :columns] + moved[:, columns : 2 * columns] + moved[:, 2 * columns :]


def load_kernel(load, place, to_faces, *faces):
    order, rows = load.shape[0], 144

    @pl.loop(0, order // rows)
    def _(step):
        at = pl.ds(pl.multiple_of(step * rows, rows), rows)
        lanes = lax.broadcasted_iota(jnp.int32, (rows, order), 1)
        to_faces[at, :] = jnp.where(place[at, :] == lanes, 1.0, 0.0).astype(BF16)

    moved = reorder_whole(to_faces[...], load[...])
    face = order // 4
    for block in range(4):
        faces[block][...] = moved[block * face : (block + 1) * face]


def setup_kernel(inverse, schur, place, inverse_high, inverse_low, schur_high, schur_low, to_local):
    rows, order = inverse.shape
    inverse_high[...], inverse_low[...] = halves(inverse[...])
    schur_high[...], schur_low[...] = halves(schur[...])
    row = lax.broadcasted_iota(jnp.int32, (rows, order), 0) + pl.program_id(0) * rows
    to_local[...] = jnp.where(place[...] == row, 1.0, 0.0).astype(BF16)


def residual_kernel(first, *refs):
    refs = list(refs)
    weights = refs.pop(0)
    basis, modes, to_local = refs[:3]
    del refs[:3]
    before = None if first else refs.pop(0)
    own, received = refs[:4], refs[4:8]
    residual, weighted, coarse_top, scaled = refs[8:]
    face = own[0].shape[0]
    for block in range(4):
        at = pl.ds(block * face, face)
        total = own[block][...] + received[block][...]
        if not first:
            total = before[at, :] - total
        residual[at, :] = total
        scaled[at, :] = total * weights[block]
    vectors = dot(to_local[...], paired(scaled[...])).astype(BF16)
    weighted[...] = vectors
    basis_high, basis_low = halves(basis[...])
    coarse = folded(dot(basis_high, vectors) + dot(basis_low, vectors))
    count = coarse.shape[0]
    coarse_top[:count, :] = coarse
    coarse_top[count:, :] = lax.dot_general(
        modes[...], coarse, (((0,), (0,)), ((), ())), precision=EXACT, preferred_element_type=F32
    )


def product_kernel(high, low, vectors, out):
    out[...] = folded(dot(high[...], vectors[...]) + dot(low[...], vectors[...]))


def pair_kernel(even, odd, out):
    count = even.shape[0] // 2
    out[:count, :] = even[:count, :]
    out[count : 2 * count, :] = odd[:count, :]
    out[2 * count :, :] = even[count:, :] + odd[count:, :]


def level_kernel(own, one, two, three, out):
    parts = (own, one, two, three)
    count = own.shape[0] // 3
    for index, part in enumerate(parts):
        out[index * 2 * count : (index + 1) * 2 * count, :] = part[: 2 * count, :]
    out[8 * count :, :] = (own[2 * count :, :] + one[2 * count :, :]) + (
        two[2 * count :, :] + three[2 * count :, :]
    )


def total_kernel(own, one, two, three, out):
    count = out.shape[0]
    at = pl.ds(own.shape[0] - count, count)
    out[...] = (own[at, :] + one[at, :]) + (two[at, :] + three[at, :])


def group_kernel(place, inverse_even, inverse_odd, own, one, two, three, out, ordered):
    high_row, row = place[0], place[1]
    width = out.shape[0]
    for by_row, part in enumerate((own, one, two, three)):
        for by_high in range(4):
            spot = (high_row ^ by_high) * 4 + (row ^ by_row)
            ordered[pl.ds(pl.multiple_of(spot * width, width), width), :] = part[
                by_high * width : (by_high + 1) * width, :
            ]
    vectors = paired(ordered[...])
    rows = jnp.concatenate([inverse_even[...], inverse_odd[...]], axis=0)
    rows_high, rows_low = halves(rows)
    out[...] = folded(dot(rows_high, vectors) + dot(rows_low, vectors))


def apex_kernel(place, top, own, one, two, three, mine, other, ordered):
    column, low_row, group = place[2], place[3], place[4]
    count = own.shape[0]
    for by_column, part in enumerate((own, one, two, three)):
        spot = column ^ by_column
        ordered[pl.ds(pl.multiple_of(spot * count, count), count), :] = part[...]
    span = 4 * count

    def share(index):
        rows = top[pl.ds(pl.multiple_of(index * count, count), count), :]
        rows = jnp.where(low_row == 0, rows[:, :span], rows[:, span:])
        return jnp.dot(rows, ordered[...], precision=EXACT, preferred_element_type=F32)

    mine[...] = share(group)
    other[...] = share(group ^ 4)


def correction_kernel(grouped, modes_even, modes_odd, mine, received, even, odd):
    count = even.shape[0]
    apex = mine[...] + received[...]
    even[...] = grouped[:count, :] + jnp.dot(
        modes_even[...], apex, precision=EXACT, preferred_element_type=F32
    )
    odd[...] = grouped[count:, :] + jnp.dot(
        modes_odd[...], apex, precision=EXACT, preferred_element_type=F32
    )


def prolong_kernel(place, weights, basis, to_faces, local_part, received, odd, *faces):
    correction = jnp.where(place[5] == 1, odd[...], received[...])
    vectors = paired(correction)
    basis_high, basis_low = halves(basis[...])
    summed = local_part[...] + folded(dot_first(basis_high, vectors) + dot_first(basis_low, vectors))
    moved = reorder(to_faces[...], summed)
    face = moved.shape[0] // 4
    for block in range(4):
        faces[block][...] = moved[block * face : (block + 1) * face] * weights[block]


def direction_kernel(first, *refs):
    refs = list(refs)
    factors, high, low, to_local, to_faces = refs[:5]
    del refs[:5]
    before, solved = (None, None) if first else (refs.pop(0), refs.pop(0))
    own, received = refs[:4], refs[4:8]
    direction, solution_out = refs[8:10]
    faces = refs[10:14]
    face = own[0].shape[0]
    for block in range(4):
        at = pl.ds(block * face, face)
        total = (own[block][...] + received[block][...]) * factors[1]
        if not first:
            total = factors[0] * before[at, :] + total
        direction[at, :] = total
        solution_out[at, :] = total if first else solved[at, :] + total
    vectors = dot(to_local[...], paired(direction[...])).astype(BF16)
    applied = folded(dot(high[...], vectors) + dot(low[...], vectors))
    moved = reorder(to_faces[...], applied)
    for block in range(4):
        faces[block][...] = moved[block * face : (block + 1) * face]


def local_kernel(to_local, values, out):
    out[...] = reorder_whole(to_local[...], values[...])


def last_kernel(to_local, before, *refs):
    own, received, (out, whole) = refs[:4], refs[4:8], refs[8:]
    face = own[0].shape[0]
    for block in range(4):
        at = pl.ds(block * face, face)
        whole[at, :] = before[at, :] - (own[block][...] + received[block][...])
    out[...] = reorder_whole(to_local[...], whole[...])


def both(pairs):
    return pairs + [(b, a) for a, b in pairs]


def shards(
    load_cases,
    schur_matrix,
    local_inverse,
    coarse_basis,
    group_inverse,
    group_modes,
    top_inverse,
    face_map,
    spectrum,
):
    order, columns = load_cases.shape
    modes = coarse_basis.shape[0]
    face = order // 4
    groups, subs = lax.axis_size("grp"), lax.axis_size("sub")
    grp, sub = lax.axis_index("grp"), lax.axis_index("sub")
    odd_core = sub % 2 == 1
    odd_group = grp % 2 == 1

    by_face = face_map.reshape(4, face)
    order_of = jnp.stack(
        [
            jnp.where(odd_core, by_face[3], by_face[2]),
            jnp.where(odd_group, by_face[1], by_face[0]),
            jnp.where(odd_group, by_face[0], by_face[1]),
            jnp.where(odd_core, by_face[2], by_face[3]),
        ]
    )
    place_row, place_column = order_of.reshape(1, order), order_of.reshape(order, 1)
    has = jnp.stack(
        [
            jnp.where(odd_core, sub < subs - 1, sub > 0),
            jnp.where(odd_group, grp < groups - 1, grp > 0),
            jnp.where(odd_group, grp > 0, grp < groups - 1),
            jnp.where(odd_core, sub > 0, sub < subs - 1),
        ]
    )
    weights = jnp.where(has, 0.5, 1.0).astype(F32)
    place = jnp.stack([sub // 8, (sub // 2) % 4, grp % 4, grp // 4, grp, sub % 2]).astype(jnp.int32)

    routes = (
        ("sub", both([(i, i + 1) for i in range(1, subs - 1, 2)])),
        ("grp", both([(i, i + 1) for i in range(1, groups - 1, 2)])),
        ("grp", both([(i, i + 1) for i in range(0, groups - 1, 2)])),
        ("sub", both([(i, i + 1) for i in range(0, subs - 1, 2)])),
    )

    def exchange(faces):
        return [lax.ppermute(part, *route) for part, route in zip(faces, routes)]

    names = ("grp", "sub")
    odds = range(1, subs, 2)

    def across_sub(x, mask):
        pairs = [(g * subs + i, g * subs + (i ^ mask)) for g in range(groups) for i in odds]
        return lax.ppermute(x, names, pairs)

    def across_grp(x, mask):
        pairs = [(g * subs + i, (g ^ mask) * subs + i) for g in range(groups) for i in odds]
        return lax.ppermute(x, names, pairs)

    def to_odd(x):
        return lax.ppermute(x, "sub", [(i - 1, i) for i in odds])

    def to_even(x):
        return lax.ppermute(x, "sub", [(i, i - 1) for i in odds])

    block = ((face, columns), F32)
    field = ((order, columns), F32)
    square = ((order, order), BF16)

    to_faces, *faces = call(
        load_kernel, [square] + [block] * 4, [("v", load_cases), ("v", place_column)]
    )
    received = exchange(faces)
    inverse_even, modes_even = to_odd(group_inverse), to_odd(group_modes)

    rows = 144
    tile = pl.BlockSpec((rows, order), lambda i: (i, 0))
    inverse_high, inverse_low, schur_high, schur_low, to_local = pl.pallas_call(
        setup_kernel,
        grid=(order // rows,),
        out_shape=[jax.ShapeDtypeStruct((order, order), BF16)] * 5,
        in_specs=[tile, tile, pl.BlockSpec((1, order), lambda i: (0, 0))],
        out_specs=[tile] * 5,
        compiler_params=pltpu.CompilerParams(vmem_limit_bytes=24 << 20),
        cost_estimate=pl.CostEstimate(flops=1 << 24, bytes_accessed=24 << 20, transcendentals=0),
    )(local_inverse, schur_matrix, place_row)

    def update(residual, faces, received):
        first = residual is None
        ins = [("s", weights), ("v", coarse_basis), ("v", group_modes), ("v", to_local)]
        ins += ([] if first else [("v", residual)]) + [("v", x) for x in faces + received]
        return call(
            functools.partial(residual_kernel, first),
            [field, ((order, 2 * columns), BF16), ((2 * modes, columns), F32)],
            ins,
            [pltpu.VMEM((order, columns), F32)],
        )

    def precondition(weighted, coarse_top):
        (local_part,) = call(
            product_kernel,
            [field],
            [("v", inverse_high), ("v", inverse_low), ("v", weighted)],
            flops=1 << 30,
        )
        even_top = to_odd(coarse_top)
        (level,) = call(
            pair_kernel, [((3 * modes, columns), F32)], [("v", even_top), ("v", coarse_top)]
        )
        others = [across_sub(level, mask) for mask in (24, 16, 8)][::-1]
        (level,) = call(
            level_kernel, [((9 * modes, columns), F32)], [("v", x) for x in [level] + others]
        )
        others = [across_sub(level, mask) for mask in (6, 4, 2)][::-1]
        gathered = [("v", x) for x in [level] + others]
        (top_term,) = call(total_kernel, [((modes, columns), F32)], gathered)
        terms = [top_term] + [across_grp(top_term, mask) for mask in (3, 2, 1)][::-1]
        (grouped,) = call(
            group_kernel,
            [((2 * modes, columns), F32)],
            [("s", place), ("v", inverse_even), ("v", group_inverse)] + gathered,
            [pltpu.VMEM((group_inverse.shape[1], columns), F32)],
            flops=1 << 26,
        )
        mine, other = call(
            apex_kernel,
            [((modes, columns), F32)] * 2,
            [("s", place), ("v", top_inverse)] + [("v", x) for x in terms],
            [pltpu.VMEM((4 * modes, columns), F32)],
        )
        theirs = across_grp(other, 4)
        even, odd = call(
            correction_kernel,
            [((modes, columns), F32)] * 2,
            [("v", x) for x in (grouped, modes_even, group_modes, mine, theirs)],
        )
        return call(
            prolong_kernel,
            [block] * 4,
            [("s", place), ("s", weights)]
            + [("v", x) for x in (coarse_basis, to_faces, local_part, to_even(even), odd)],
        )

    centre = 0.5 * (spectrum[0] + spectrum[1])
    half_width = 0.5 * (spectrum[1] - spectrum[0])
    rho = half_width / centre
    factors = jnp.stack([jnp.zeros((), F32), 1.0 / centre])
    residual = direction = solved = None
    for step in range(ITERS):
        residual, weighted, coarse_top = update(residual, faces, received)
        faces = precondition(weighted, coarse_top)
        received = exchange(faces)
        ins = [("s", factors)]
        ins += [("v", x) for x in (schur_high, schur_low, to_local, to_faces)]
        ins += [] if step == 0 else [("v", direction), ("v", solved)]
        direction, solved, *faces = call(
            functools.partial(direction_kernel, step == 0),
            [field, field] + [block] * 4,
            ins + [("v", x) for x in faces + received],
            flops=1 << 30,
        )
        received = exchange(faces)
        rho_next = 1.0 / (2.0 * centre / half_width - rho)
        factors = jnp.stack([rho_next * rho, 2.0 * rho_next / half_width])
        rho = rho_next
    (displacement,) = call(local_kernel, [field], [("v", to_local), ("v", solved)], flops=1 << 28)
    (remainder,) = call(
        last_kernel,
        [field],
        [("v", to_local), ("v", residual)] + [("v", x) for x in faces + received],
        [pltpu.VMEM((order, columns), F32)],
    )
    return displacement, remainder


def solution(mesh):
    placed = (
        P(("grp", "sub"), None),
        P(("grp", "sub"), None),
        P(("grp", "sub"), None),
        P(("grp", "sub"), None),
        P(("grp", "sub"), None),
        P(("grp", "sub"), None),
        P(),
        P(("grp", "sub"), None),
        P(),
    )
    return jax.shard_map(
        shards,
        mesh=mesh,
        in_specs=placed,
        out_specs=(P(("grp", "sub"), None), P(("grp", "sub"), None)),
        check_vma=False,
    )
```

```python
import functools

import jax
import jax.numpy as jnp
from jax import lax
from jax.experimental import pallas as pl
from jax.experimental.pallas import tpu as pltpu
from jax.sharding import PartitionSpec as P

ITERS = 3
F32, BF16 = jnp.float32, jnp.bfloat16
EXACT = lax.Precision.HIGHEST
VMEM = pl.BlockSpec(memory_space=pltpu.VMEM)
SMEM = pl.BlockSpec(memory_space=pltpu.SMEM)
LARGE = 8 << 20


def call(kernel, outs, ins, scratch=(), limit=2 << 20, flops=1 << 20):
    specs = [SMEM if kind == "s" else VMEM for kind, _ in ins]
    results = pl.pallas_call(
        kernel,
        out_shape=[jax.ShapeDtypeStruct(shape, dtype) for shape, dtype in outs],
        in_specs=specs,
        out_specs=[VMEM] * len(outs),
        scratch_shapes=list(scratch),
        compiler_params=pltpu.CompilerParams(vmem_limit_bytes=limit),
        cost_estimate=pl.CostEstimate(flops=flops, bytes_accessed=1 << 20, transcendentals=0),
    )(*[array for _, array in ins])
    return list(results)


def halves(x):
    high = x.astype(BF16)
    return high, (x - high.astype(F32)).astype(BF16)


def paired(x):
    return jnp.concatenate(halves(x), axis=1)


def dot(a, b):
    return jnp.dot(a, b, preferred_element_type=F32)


def dot_first(a, b):
    return lax.dot_general(a, b, (((0,), (0,)), ((), ())), preferred_element_type=F32)


def folded(x):
    columns = x.shape[1] // 2
    return x[:, :columns] + x[:, columns:]


def blocks(order, count=4):
    rows = order // count
    return [pl.ds(index * rows, rows) for index in range(count)]


def put_pair(out, at, x):
    columns = x.shape[1]
    out[at, :columns], out[at, columns:] = halves(x)


def put_three(out, x):
    columns = x.shape[1]
    high, low = halves(x)
    out[:, :columns], out[:, columns : 2 * columns] = high, low
    out[:, 2 * columns :] = (x - high.astype(F32) - low.astype(F32)).astype(BF16)


def sum_three(x):
    columns = x.shape[1] // 3
    return x[:, :columns] + x[:, columns : 2 * columns] + x[:, 2 * columns :]


def arrived(flags, block, received):
    return jnp.where(flags[4 + block] > 0.5, received[block][...], 0.0)


def load_kernel(load, place, to_faces, f0, f1, f2, f3, parts):
    order, rows = load.shape[0], 144

    @pl.loop(0, order // rows)
    def _(step):
        at = pl.ds(pl.multiple_of(step * rows, rows), rows)
        lanes = lax.broadcasted_iota(jnp.int32, (rows, order), 1)
        to_faces[at, :] = jnp.where(place[at, :] == lanes, 1.0, 0.0).astype(BF16)

    put_three(parts, load[...])
    for at, out in zip(blocks(order), (f0, f1, f2, f3)):
        out[...] = sum_three(dot(to_faces[at, :], parts[...]))


def split_kernel(matrix, high, low):
    rows = 144

    @pl.loop(0, matrix.shape[0] // rows)
    def _(step):
        at = pl.ds(pl.multiple_of(step * rows, rows), rows)
        high[at, :], low[at, :] = halves(matrix[at, :])


def onehot_kernel(place, to_local):
    order, rows = place.shape[1], 144

    @pl.loop(0, order // rows)
    def _(step):
        at = pl.ds(pl.multiple_of(step * rows, rows), rows)
        row = lax.broadcasted_iota(jnp.int32, (rows, order), 0) + step * rows
        to_local[at, :] = jnp.where(place[...] == row, 1.0, 0.0).astype(BF16)


def residual_kernel(first, *refs):
    refs = list(refs)
    flags = refs.pop(0)
    basis, modes, to_local = refs[:3]
    del refs[:3]
    before = None if first else refs.pop(0)
    own, received = refs[:4], refs[4:8]
    residual, weighted, coarse_top, parts = refs[8:]
    order = residual.shape[0]
    for block, at in enumerate(blocks(order)):
        total = own[block][...] + arrived(flags, block, received)
        if not first:
            total = before[at, :] - total
        residual[at, :] = total
        put_pair(parts, at, total * flags[block])
    for at in blocks(order):
        weighted[at, :] = dot(to_local[at, :], parts[...]).astype(BF16)
    basis_high, basis_low = halves(basis[...])
    coarse = folded(dot(basis_high, weighted[...]) + dot(basis_low, weighted[...]))
    count = coarse.shape[0]
    coarse_top[:count, :] = coarse
    coarse_top[count:, :] = lax.dot_general(
        modes[...], coarse, (((0,), (0,)), ((), ())), precision=EXACT, preferred_element_type=F32
    )


def product_kernel(high, low, vectors, out):
    for at in blocks(out.shape[0]):
        out[at, :] = folded(dot(high[at, :], vectors[...]) + dot(low[at, :], vectors[...]))


def level_kernel(count, own, one, two, three, out):
    parts = (own, one, two, three)
    size = own.shape[0] - count
    for index, part in enumerate(parts):
        out[index * size : (index + 1) * size, :] = part[:size, :]
    out[4 * size :, :] = (own[size:, :] + one[size:, :]) + (two[size:, :] + three[size:, :])


def total_kernel(own, other, out):
    count = out.shape[0]
    at = pl.ds(own.shape[0] - count, count)
    out[...] = own[at, :] + other[at, :]


def group_kernel(place, inverse, own, other, out, vectors):
    high_row, row, core = place[0], place[1], place[5]
    width, columns = out.shape
    for by_core, part in enumerate((own, other)):
        for by_row in range(4):
            for by_high in range(4):
                spot = ((high_row ^ by_high) * 4 + (row ^ by_row)) * 2 + (core ^ by_core)
                at = pl.ds(pl.multiple_of(spot * width, width), width)
                source = (by_row * 4 + by_high) * width
                put_pair(vectors, at, part[source : source + width, :])
    rows_high, rows_low = halves(inverse[...])
    out[...] = folded(dot(rows_high, vectors[...]) + dot(rows_low, vectors[...]))


def apex_kernel(place, top, own, one, two, three, mine, other, ordered):
    column, low_row, group = place[2], place[3], place[4]
    count = own.shape[0]
    for by_column, part in enumerate((own, one, two, three)):
        spot = column ^ by_column
        ordered[pl.ds(pl.multiple_of(spot * count, count), count), :] = part[...]
    span = 4 * count

    def share(index):
        rows = top[pl.ds(pl.multiple_of(index * count, count), count), :]
        rows = jnp.where(low_row == 0, rows[:, :span], rows[:, span:])
        return jnp.dot(rows, ordered[...], precision=EXACT, preferred_element_type=F32)

    mine[...] = share(group)
    other[...] = share(group ^ 4)


def prolong_kernel(
    flags, basis, modes, to_faces, local_part, grouped, mine, theirs, f0, f1, f2, f3, parts
):
    apex = mine[...] + theirs[...]
    correction = grouped[...] + jnp.dot(
        modes[...], apex, precision=EXACT, preferred_element_type=F32
    )
    vectors = paired(correction)
    order = local_part.shape[0]
    for at in blocks(order, 3):
        high, low = halves(basis[:, at])
        lifted = folded(dot_first(high, vectors) + dot_first(low, vectors))
        put_pair(parts, at, local_part[at, :] + lifted)
    for block, (at, out) in enumerate(zip(blocks(order), (f0, f1, f2, f3))):
        out[...] = folded(dot(to_faces[at, :], parts[...])) * flags[block]


def direction_kernel(step, *refs):
    refs, first = list(refs), step == 0
    flags, high, low, to_local, to_faces = refs[:5]
    del refs[:5]
    old, new = flags[8 + 2 * step], flags[9 + 2 * step]
    before, solved = (None, None) if first else (refs.pop(0), refs.pop(0))
    own, received = refs[:4], refs[4:8]
    direction, solution_out = refs[8:10]
    faces, (parts, vectors) = refs[10:14], refs[14:]
    order = direction.shape[0]
    for block, at in enumerate(blocks(order)):
        total = (own[block][...] + arrived(flags, block, received)) * new
        if not first:
            total = old * before[at, :] + total
        direction[at, :] = total
        solution_out[at, :] = total if first else solved[at, :] + total
        put_pair(parts, at, total)
    for at in blocks(order):
        vectors[at, :] = dot(to_local[at, :], parts[...]).astype(BF16)
    for at in blocks(order):
        put_pair(parts, at, folded(dot(high[at, :], vectors[...]) + dot(low[at, :], vectors[...])))
    for at, out in zip(blocks(order), faces):
        out[...] = folded(dot(to_faces[at, :], parts[...]))


def local_kernel(to_local, values, out, parts):
    put_three(parts, values[...])
    for at in blocks(out.shape[0]):
        out[at, :] = sum_three(dot(to_local[at, :], parts[...]))


def last_kernel(flags, to_local, before, *refs):
    own, received, (out, whole, parts) = refs[:4], refs[4:8], refs[8:]
    for block, at in enumerate(blocks(out.shape[0])):
        whole[at, :] = before[at, :] - (own[block][...] + arrived(flags, block, received))
    local_kernel(to_local, whole, out, parts)


def both(pairs):
    return pairs + [(b, a) for a, b in pairs]


def shards(
    load_cases,
    schur_matrix,
    local_inverse,
    coarse_basis,
    group_inverse,
    group_modes,
    top_inverse,
    face_map,
    spectrum,
):
    order, columns = load_cases.shape
    modes = coarse_basis.shape[0]
    face = order // 4
    groups, subs = lax.axis_size("grp"), lax.axis_size("sub")
    grp, sub = lax.axis_index("grp"), lax.axis_index("sub")
    odd_core = (sub & 1) == 1
    odd_group = (grp & 1) == 1

    by_face = face_map.reshape(4, face)
    order_of = jnp.stack(
        [
            jnp.where(odd_core, by_face[3], by_face[2]),
            jnp.where(odd_group, by_face[1], by_face[0]),
            jnp.where(odd_group, by_face[0], by_face[1]),
            jnp.where(odd_core, by_face[2], by_face[3]),
        ]
    )
    place_row, place_column = order_of.reshape(1, order), order_of.reshape(order, 1)
    has = jnp.stack(
        [
            jnp.where(odd_core, sub < subs - 1, sub > 0),
            jnp.where(odd_group, grp < groups - 1, grp > 0),
            jnp.where(odd_group, grp > 0, grp < groups - 1),
            jnp.where(odd_core, sub > 0, sub < subs - 1),
        ]
    )
    place = jnp.stack([sub >> 3, (sub >> 1) & 3, grp & 3, grp >> 2, grp, sub & 1]).astype(jnp.int32)

    centre = 0.5 * (spectrum[0] + spectrum[1])
    half_width = 0.5 * (spectrum[1] - spectrum[0])
    rho = half_width / centre
    factors = [jnp.zeros((), F32), 1.0 / centre]
    for _ in range(ITERS - 1):
        rho_next = 1.0 / (2.0 * centre / half_width - rho)
        factors += [rho_next * rho, 2.0 * rho_next / half_width]
        rho = rho_next
    numbers = jnp.stack([*jnp.where(has, 0.5, 1.0), *has.astype(F32), *factors]).astype(F32)
    load_cases, place_row, place_column, place, numbers = lax.optimization_barrier(
        (load_cases, place_row, place_column, place, numbers)
    )

    routes = (
        ("sub", both([(i, (i + 1) % subs) for i in range(1, subs, 2)])),
        ("grp", both([(i, (i + 1) % groups) for i in range(1, groups, 2)])),
        ("grp", both([(i, i + 1) for i in range(0, groups, 2)])),
        ("sub", both([(i, i + 1) for i in range(0, subs, 2)])),
    )

    def exchange(faces):
        return [lax.ppermute(part, *route) for part, route in zip(faces, routes)]

    def across_sub(x, mask):
        return lax.ppermute(x, "sub", [(i, i ^ mask) for i in range(subs)])

    def across_grp(x, mask):
        return lax.ppermute(x, "grp", [(i, i ^ mask) for i in range(groups)])

    block = ((face, columns), F32)
    field = ((order, columns), F32)
    square = ((order, order), BF16)
    pair = pltpu.VMEM((order, 2 * columns), BF16)
    three = pltpu.VMEM((order, 3 * columns), BF16)

    to_faces, *faces = call(
        load_kernel,
        [square] + [block] * 4,
        [("v", load_cases), ("v", place_column)],
        [three],
        LARGE,
    )
    received = exchange(faces)
    (to_local,) = call(onehot_kernel, [square], [("v", place_row)])
    inverse_high, inverse_low = call(split_kernel, [square] * 2, [("v", local_inverse)])
    schur_high, schur_low = call(split_kernel, [square] * 2, [("v", schur_matrix)])

    def update(residual, faces, received):
        first = residual is None
        ins = [("s", numbers), ("v", coarse_basis), ("v", group_modes), ("v", to_local)]
        ins += ([] if first else [("v", residual)]) + [("v", x) for x in faces + received]
        return call(
            functools.partial(residual_kernel, first),
            [field, ((order, 2 * columns), BF16), ((2 * modes, columns), F32)],
            ins,
            [pair],
            LARGE,
        )

    def precondition(weighted, coarse_top):
        (local_part,) = call(
            product_kernel,
            [field],
            [("v", inverse_high), ("v", inverse_low), ("v", weighted)],
            limit=LARGE,
            flops=1 << 30,
        )
        others = [across_sub(coarse_top, mask) for mask in (8, 16, 24)]
        others, local_part = lax.optimization_barrier((others, local_part))
        (level,) = call(
            functools.partial(level_kernel, modes),
            [((5 * modes, columns), F32)],
            [("v", x) for x in [coarse_top] + others],
        )
        others = [across_sub(level, mask) for mask in (2, 4, 6)]
        (level,) = call(
            functools.partial(level_kernel, modes),
            [((17 * modes, columns), F32)],
            [("v", x) for x in [level] + others],
        )
        gathered = [("v", level), ("v", across_sub(level, 1))]
        (top_term,) = call(total_kernel, [((modes, columns), F32)], gathered)
        (grouped,) = call(
            group_kernel,
            [((modes, columns), F32)],
            [("s", place), ("v", group_inverse)] + gathered,
            [pltpu.VMEM((group_inverse.shape[1], 2 * columns), BF16)],
            flops=1 << 26,
        )
        others = [across_grp(top_term, mask) for mask in (1, 2, 3)]
        others, grouped = lax.optimization_barrier((others, grouped))
        mine, other = call(
            apex_kernel,
            [((modes, columns), F32)] * 2,
            [("s", place), ("v", top_inverse)] + [("v", x) for x in [top_term] + others],
            [pltpu.VMEM((4 * modes, columns), F32)],
        )
        ins = (coarse_basis, group_modes, to_faces, local_part, grouped, mine, across_grp(other, 4))
        return call(
            prolong_kernel,
            [block] * 4,
            [("s", numbers)] + [("v", x) for x in ins],
            [pair],
            LARGE,
        )

    residual = direction = solved = None
    for step in range(ITERS):
        residual, weighted, coarse_top = update(residual, faces, received)
        faces = precondition(weighted, coarse_top)
        received = exchange(faces)
        ins = [("s", numbers)]
        ins += [("v", x) for x in (schur_high, schur_low, to_local, to_faces)]
        ins += [] if step == 0 else [("v", direction), ("v", solved)]
        direction, solved, *faces = call(
            functools.partial(direction_kernel, step),
            [field, field] + [block] * 4,
            ins + [("v", x) for x in faces + received],
            [pair] * 2,
            LARGE,
            flops=1 << 30,
        )
        received = exchange(faces)
    (displacement,) = call(
        local_kernel, [field], [("v", to_local), ("v", solved)], [three], LARGE, flops=1 << 28
    )
    (remainder,) = call(
        last_kernel,
        [field],
        [("s", numbers), ("v", to_local), ("v", residual)] + [("v", x) for x in faces + received],
        [pltpu.VMEM((order, columns), F32), three],
        LARGE,
    )
    return displacement, remainder


def solution(mesh):
    placed = (
        P(("grp", "sub"), None),
        P(("grp", "sub"), None),
        P(("grp", "sub"), None),
        P(("grp", "sub"), None),
        P(("grp", "sub"), None),
        P(("grp", "sub"), None),
        P(),
        P(("grp", "sub"), None),
        P(),
    )
    return jax.shard_map(
        shards,
        mesh=mesh,
        in_specs=placed,
        out_specs=(P(("grp", "sub"), None), P(("grp", "sub"), None)),
        check_vma=False,
    )
```

```python
import functools

import jax
import jax.numpy as jnp
from jax import lax
from jax.experimental import pallas as pl
from jax.experimental.pallas import tpu as pltpu
from jax.sharding import PartitionSpec as P

ITERS = 3
F32, BF16 = jnp.float32, jnp.bfloat16
EXACT = lax.Precision.HIGHEST
VMEM = pl.BlockSpec(memory_space=pltpu.VMEM)
SMEM = pl.BlockSpec(memory_space=pltpu.SMEM)
LARGE = 8 << 20


def call(kernel, outs, ins, scratch=(), limit=2 << 20, flops=1 << 20):
    specs = [SMEM if kind == "s" else VMEM for kind, _ in ins]
    results = pl.pallas_call(
        kernel,
        out_shape=[jax.ShapeDtypeStruct(shape, dtype) for shape, dtype in outs],
        in_specs=specs,
        out_specs=[VMEM] * len(outs),
        scratch_shapes=list(scratch),
        compiler_params=pltpu.CompilerParams(vmem_limit_bytes=limit),
        cost_estimate=pl.CostEstimate(flops=flops, bytes_accessed=1 << 20, transcendentals=0),
    )(*[array for _, array in ins])
    return list(results)


def halves(x):
    high = x.astype(BF16)
    return high, (x - high.astype(F32)).astype(BF16)


def paired(x):
    return jnp.concatenate(halves(x), axis=1)


def dot(a, b):
    return jnp.dot(a, b, preferred_element_type=F32)


def dot_first(a, b):
    return lax.dot_general(a, b, (((0,), (0,)), ((), ())), preferred_element_type=F32)


def folded(x):
    columns = x.shape[1] // 2
    return x[:, :columns] + x[:, columns:]


def blocks(order, count=4):
    rows = order // count
    return [pl.ds(index * rows, rows) for index in range(count)]


def put_pair(out, at, x):
    columns = x.shape[1]
    out[at, :columns], out[at, columns:] = halves(x)


def put_three(out, x):
    columns = x.shape[1]
    high, low = halves(x)
    out[:, :columns], out[:, columns : 2 * columns] = high, low
    out[:, 2 * columns :] = (x - high.astype(F32) - low.astype(F32)).astype(BF16)


def sum_three(x):
    columns = x.shape[1] // 3
    return x[:, :columns] + x[:, columns : 2 * columns] + x[:, 2 * columns :]


def arrived(flags, block, received):
    return jnp.where(flags[0, 4 + block] > 0.5, received[block][...], 0.0)


def numbers_kernel(spectrum, numbers, place):
    groups, subs = lax.axis_size("grp"), lax.axis_size("sub")
    grp, sub = lax.axis_index("grp"), lax.axis_index("sub")
    lanes = lax.broadcasted_iota(jnp.int32, (1, 128), 1)

    def lined(values, zero):
        out = jnp.full((1, 128), zero)
        for index, value in enumerate(values):
            out = jnp.where(lanes == index, value, out)
        return out

    low, high = jnp.full((1, 128), spectrum[0]), jnp.full((1, 128), spectrum[1])
    centre, half_width = 0.5 * (low + high), 0.5 * (high - low)
    rho = half_width / centre
    factors = [0.0, 1.0 / centre]
    for _ in range(ITERS - 1):
        rho_next = 1.0 / (2.0 * centre / half_width - rho)
        factors += [rho_next * rho, 2.0 * rho_next / half_width]
        rho = rho_next
    odd_core, odd_group = (sub & 1) == 1, (grp & 1) == 1
    none = [
        sub == jnp.where(odd_core, subs - 1, 0),
        grp == jnp.where(odd_group, groups - 1, 0),
        grp == jnp.where(odd_group, 0, groups - 1),
        sub == jnp.where(odd_core, 0, subs - 1),
    ]
    weights = [jnp.where(x, 1.0, 0.5) for x in none]
    has = [jnp.where(x, 0.0, 1.0) for x in none]
    numbers[...] = lined(weights + has + factors, 0.0)
    place[...] = lined([sub >> 3, (sub >> 1) & 3, grp & 3, grp >> 2, grp, sub & 1], 0)


def load_kernel(load, place, to_faces, f0, f1, f2, f3, parts):
    order, rows = load.shape[0], 144

    @pl.loop(0, order // rows)
    def _(step):
        at = pl.ds(pl.multiple_of(step * rows, rows), rows)
        lanes = lax.broadcasted_iota(jnp.int32, (rows, order), 1)
        to_faces[at, :] = jnp.where(place[at, :] == lanes, 1.0, 0.0).astype(BF16)

    put_three(parts, load[...])
    for at, out in zip(blocks(order), (f0, f1, f2, f3)):
        out[...] = sum_three(dot(to_faces[at, :], parts[...]))


def basis_kernel(basis, to_local, to_faces, rows, columns):
    both_parts = jnp.concatenate(halves(basis[...]), axis=0)
    rows[...] = dot(both_parts, to_local[...]).astype(BF16)
    columns[...] = lax.dot_general(
        to_faces[...], both_parts, (((1,), (1,)), ((), ())), preferred_element_type=F32
    ).astype(BF16)


def split_kernel(matrix, high, low):
    rows = 144

    @pl.loop(0, matrix.shape[0] // rows)
    def _(step):
        at = pl.ds(pl.multiple_of(step * rows, rows), rows)
        high[at, :], low[at, :] = halves(matrix[at, :])


def onehot_kernel(place, to_local):
    order, rows = place.shape[1], 144

    @pl.loop(0, order // rows)
    def _(step):
        at = pl.ds(pl.multiple_of(step * rows, rows), rows)
        row = lax.broadcasted_iota(jnp.int32, (rows, order), 0) + step * rows
        to_local[at, :] = jnp.where(place[...] == row, 1.0, 0.0).astype(BF16)


def residual_kernel(first, *refs):
    refs = list(refs)
    flags, basis, modes = refs[:3]
    del refs[:3]
    before = None if first else refs.pop(0)
    own, received = refs[:4], refs[4:8]
    residual, parts, coarse_top = refs[8:]
    order = residual.shape[0]
    for block, at in enumerate(blocks(order)):
        total = own[block][...] + arrived(flags, block, received)
        if not first:
            total = before[at, :] - total
        residual[at, :] = total
        put_pair(parts, at, total * flags[0, block])
    product = folded(dot(basis[...], parts[...]))
    count = product.shape[0] // 2
    coarse = product[:count, :] + product[count:, :]
    coarse_top[:count, :] = coarse
    coarse_top[count:, :] = lax.dot_general(
        modes[...], coarse, (((0,), (0,)), ((), ())), precision=EXACT, preferred_element_type=F32
    )


def apply(high, low, to_local, to_faces, parts, vectors, results, outs):
    order = parts.shape[0]
    for at in blocks(order):
        vectors[at, :] = dot(to_local[at, :], parts[...]).astype(BF16)
    for at in blocks(order):
        product = folded(dot(high[at, :], vectors[...]) + dot(low[at, :], vectors[...]))
        put_pair(results, at, product)
    for at, out in zip(blocks(order), outs):
        out[...] = folded(dot(to_faces[at, :], results[...]))


def product_kernel(high, low, to_local, to_faces, parts, o0, o1, o2, o3, vectors, results):
    apply(high, low, to_local, to_faces, parts, vectors, results, (o0, o1, o2, o3))


def level_kernel(count, own, one, two, three, out):
    parts = (own, one, two, three)
    size = own.shape[0] - count
    for index, part in enumerate(parts):
        out[index * size : (index + 1) * size, :] = part[:size, :]
    out[4 * size :, :] = (own[size:, :] + one[size:, :]) + (two[size:, :] + three[size:, :])


def total_kernel(own, other, out):
    count = out.shape[0]
    at = pl.ds(own.shape[0] - count, count)
    out[...] = own[at, :] + other[at, :]


def group_kernel(place, inverse, own, other, out, vectors):
    high_row, row, core = place[0, 0], place[0, 1], place[0, 5]
    width, columns = out.shape
    for by_core, part in enumerate((own, other)):
        for by_row in range(4):
            for by_high in range(4):
                spot = ((high_row ^ by_high) * 4 + (row ^ by_row)) * 2 + (core ^ by_core)
                at = pl.ds(pl.multiple_of(spot * width, width), width)
                source = (by_row * 4 + by_high) * width
                put_pair(vectors, at, part[source : source + width, :])
    rows_high, rows_low = halves(inverse[...])
    out[...] = folded(dot(rows_high, vectors[...]) + dot(rows_low, vectors[...]))


def apex_rows(place, top, index, count):
    rows = top[pl.ds(pl.multiple_of(index * count, count), count), :]
    span = rows.shape[1] // 2
    return jnp.where(place[0, 3] == 0, rows[:, :span], rows[:, span:])


def apex_kernel(place, top, own, one, two, three, other, ordered):
    count = own.shape[0]
    for by_column, part in enumerate((own, one, two, three)):
        spot = place[0, 2] ^ by_column
        ordered[pl.ds(pl.multiple_of(spot * count, count), count), :] = part[...]
    rows = apex_rows(place, top, place[0, 4] ^ 4, count)
    other[...] = jnp.dot(rows, ordered[...], precision=EXACT, preferred_element_type=F32)


def partial_kernel(place, top, modes, ordered, grouped, out):
    rows = apex_rows(place, top, place[0, 4], grouped.shape[0])
    mine = jnp.dot(rows, ordered[...], precision=EXACT, preferred_element_type=F32)
    out[...] = grouped[...] + jnp.dot(
        modes[...], mine, precision=EXACT, preferred_element_type=F32
    )


def prolong_kernel(flags, basis, modes, partial, theirs, l0, l1, l2, l3, f0, f1, f2, f3):
    correction = partial[...] + jnp.dot(
        modes[...], theirs[...], precision=EXACT, preferred_element_type=F32
    )
    vectors = paired(correction)
    vectors = jnp.concatenate([vectors, vectors], axis=0)
    sources, outs = (l0, l1, l2, l3), (f0, f1, f2, f3)
    for block, at in enumerate(blocks(basis.shape[0])):
        lifted = folded(dot(basis[at, :], vectors))
        outs[block][...] = (sources[block][...] + lifted) * flags[0, block]


def direction_kernel(step, *refs):
    refs, first = list(refs), step == 0
    flags, high, low, to_local, to_faces = refs[:5]
    del refs[:5]
    old, new = flags[0, 8 + 2 * step], flags[0, 9 + 2 * step]
    before, solved = (None, None) if first else (refs.pop(0), refs.pop(0))
    own, received = refs[:4], refs[4:8]
    direction, solution_out = refs[8:10]
    faces, (parts, vectors) = refs[10:14], refs[14:]
    order = direction.shape[0]
    for block, at in enumerate(blocks(order)):
        total = (own[block][...] + arrived(flags, block, received)) * new
        if not first:
            total = old * before[at, :] + total
        direction[at, :] = total
        solution_out[at, :] = total if first else solved[at, :] + total
        put_pair(parts, at, total)
    apply(high, low, to_local, to_faces, parts, vectors, parts, faces)


def local_kernel(to_local, values, out, parts):
    put_three(parts, values[...])
    for at in blocks(out.shape[0]):
        out[at, :] = sum_three(dot(to_local[at, :], parts[...]))


def last_kernel(flags, to_local, before, *refs):
    own, received, (out, whole, parts) = refs[:4], refs[4:8], refs[8:]
    for block, at in enumerate(blocks(out.shape[0])):
        whole[at, :] = before[at, :] - (own[block][...] + arrived(flags, block, received))
    local_kernel(to_local, whole, out, parts)


def both(pairs):
    return pairs + [(b, a) for a, b in pairs]


def shards(
    load_cases,
    schur_matrix,
    local_inverse,
    coarse_basis,
    group_inverse,
    group_modes,
    top_inverse,
    face_map,
    spectrum,
):
    order, columns = load_cases.shape
    modes = coarse_basis.shape[0]
    face = order // 4
    groups, subs = lax.axis_size("grp"), lax.axis_size("sub")
    grp, sub = lax.axis_index("grp"), lax.axis_index("sub")
    odd_core = (sub & 1) == 1
    odd_group = (grp & 1) == 1

    by_face = face_map.reshape(4, face)
    order_of = jnp.stack(
        [
            jnp.where(odd_core, by_face[3], by_face[2]),
            jnp.where(odd_group, by_face[1], by_face[0]),
            jnp.where(odd_group, by_face[0], by_face[1]),
            jnp.where(odd_core, by_face[2], by_face[3]),
        ]
    )
    place_row, place_column = order_of.reshape(1, order), order_of.reshape(order, 1)
    numbers, place = call(
        numbers_kernel, [((1, 128), F32), ((1, 128), jnp.int32)], [("s", spectrum)]
    )
    load_cases, place_row, place_column, place, numbers = lax.optimization_barrier(
        (load_cases, place_row, place_column, place, numbers)
    )

    routes = (
        ("sub", both([(i, (i + 1) % subs) for i in range(1, subs, 2)])),
        ("grp", both([(i, (i + 1) % groups) for i in range(1, groups, 2)])),
        ("grp", both([(i, i + 1) for i in range(0, groups, 2)])),
        ("sub", both([(i, i + 1) for i in range(0, subs, 2)])),
    )

    def exchange(faces):
        return [lax.ppermute(part, *route) for part, route in zip(faces, routes)]

    def across_sub(x, mask):
        return lax.ppermute(x, "sub", [(i, i ^ mask) for i in range(subs)])

    def across_grp(x, mask):
        return lax.ppermute(x, "grp", [(i, i ^ mask) for i in range(groups)])

    block = ((face, columns), F32)
    field = ((order, columns), F32)
    square = ((order, order), BF16)
    pair = pltpu.VMEM((order, 2 * columns), BF16)
    three = pltpu.VMEM((order, 3 * columns), BF16)

    to_faces, *faces = call(
        load_kernel,
        [square] + [block] * 4,
        [("v", load_cases), ("v", place_column)],
        [three],
        LARGE,
    )
    received = exchange(faces)
    (to_local,) = call(onehot_kernel, [square], [("v", place_row)])
    basis_rows, basis_columns = call(
        basis_kernel,
        [((2 * modes, order), BF16), ((order, 2 * modes), BF16)],
        [("v", coarse_basis), ("v", to_local), ("v", to_faces)],
        limit=LARGE,
    )
    inverse_high, inverse_low = call(split_kernel, [square] * 2, [("v", local_inverse)])
    schur_high, schur_low = call(split_kernel, [square] * 2, [("v", schur_matrix)])

    def update(residual, faces, received):
        first = residual is None
        ins = [("s", numbers), ("v", basis_rows), ("v", group_modes)]
        ins += ([] if first else [("v", residual)]) + [("v", x) for x in faces + received]
        return call(
            functools.partial(residual_kernel, first),
            [field, ((order, 2 * columns), BF16), ((2 * modes, columns), F32)],
            ins,
            limit=LARGE,
        )

    def precondition(weighted, coarse_top):
        local_part = call(
            product_kernel,
            [block] * 4,
            [("v", x) for x in (inverse_high, inverse_low, to_local, to_faces, weighted)],
            [pair] * 2,
            LARGE,
            flops=1 << 30,
        )
        others = [across_sub(coarse_top, mask) for mask in (8, 16, 24)]
        others, local_part = lax.optimization_barrier((others, local_part))
        (level,) = call(
            functools.partial(level_kernel, modes),
            [((5 * modes, columns), F32)],
            [("v", x) for x in [coarse_top] + others],
        )
        others = [across_sub(level, mask) for mask in (2, 4, 6)]
        (level,) = call(
            functools.partial(level_kernel, modes),
            [((17 * modes, columns), F32)],
            [("v", x) for x in [level] + others],
        )
        gathered = [("v", level), ("v", across_sub(level, 1))]
        (top_term,) = call(total_kernel, [((modes, columns), F32)], gathered)
        (grouped,) = call(
            group_kernel,
            [((modes, columns), F32)],
            [("s", place), ("v", group_inverse)] + gathered,
            [pltpu.VMEM((group_inverse.shape[1], 2 * columns), BF16)],
            flops=1 << 26,
        )
        others = [across_grp(top_term, mask) for mask in (1, 2, 3)]
        others, grouped = lax.optimization_barrier((others, grouped))
        other, ordered = call(
            apex_kernel,
            [((modes, columns), F32), ((4 * modes, columns), F32)],
            [("s", place), ("v", top_inverse)] + [("v", x) for x in [top_term] + others],
        )
        theirs = across_grp(other, 4)
        (partial,) = call(
            partial_kernel,
            [((modes, columns), F32)],
            [("s", place)] + [("v", x) for x in (top_inverse, group_modes, ordered, grouped)],
        )
        theirs, partial = lax.optimization_barrier((theirs, partial))
        ins = [basis_columns, group_modes, partial, theirs] + local_part
        return call(
            prolong_kernel,
            [block] * 4,
            [("s", numbers)] + [("v", x) for x in ins],
            limit=LARGE,
        )

    residual = direction = solved = None
    for step in range(ITERS):
        residual, weighted, coarse_top = update(residual, faces, received)
        faces = precondition(weighted, coarse_top)
        received = exchange(faces)
        ins = [("s", numbers)]
        ins += [("v", x) for x in (schur_high, schur_low, to_local, to_faces)]
        ins += [] if step == 0 else [("v", direction), ("v", solved)]
        direction, solved, *faces = call(
            functools.partial(direction_kernel, step),
            [field, field] + [block] * 4,
            ins + [("v", x) for x in faces + received],
            [pair] * 2,
            LARGE,
            flops=1 << 30,
        )
        received = exchange(faces)
    (displacement,) = call(
        local_kernel, [field], [("v", to_local), ("v", solved)], [three], LARGE, flops=1 << 28
    )
    (remainder,) = call(
        last_kernel,
        [field],
        [("s", numbers), ("v", to_local), ("v", residual)] + [("v", x) for x in faces + received],
        [pltpu.VMEM((order, columns), F32), three],
        LARGE,
    )
    return displacement, remainder


def solution(mesh):
    placed = (
        P(("grp", "sub"), None),
        P(("grp", "sub"), None),
        P(("grp", "sub"), None),
        P(("grp", "sub"), None),
        P(("grp", "sub"), None),
        P(("grp", "sub"), None),
        P(),
        P(("grp", "sub"), None),
        P(),
    )
    return jax.shard_map(
        shards,
        mesh=mesh,
        in_specs=placed,
        out_specs=(P(("grp", "sub"), None), P(("grp", "sub"), None)),
        check_vma=False,
    )
```

```python
import functools

import jax
import jax.numpy as jnp
from jax import lax
from jax.experimental import pallas as pl
from jax.experimental.pallas import tpu as pltpu
from jax.sharding import PartitionSpec as P

ITERS = 3
F32, BF16 = jnp.float32, jnp.bfloat16
EXACT = lax.Precision.HIGHEST
VMEM = pl.BlockSpec(memory_space=pltpu.VMEM)
SMEM = pl.BlockSpec(memory_space=pltpu.SMEM)
LARGE = 8 << 20


def call(kernel, outs, ins, scratch=(), limit=2 << 20, flops=1 << 20):
    spaces = {"s": SMEM, "v": VMEM, "a": pl.BlockSpec(memory_space=pl.ANY)}
    specs = [spaces[kind] for kind, _ in ins]
    results = pl.pallas_call(
        kernel,
        out_shape=[jax.ShapeDtypeStruct(shape, dtype) for shape, dtype in outs],
        in_specs=specs,
        out_specs=[VMEM] * len(outs),
        scratch_shapes=list(scratch),
        compiler_params=pltpu.CompilerParams(vmem_limit_bytes=limit),
        cost_estimate=pl.CostEstimate(flops=flops, bytes_accessed=1 << 20, transcendentals=0),
    )(*[array for _, array in ins])
    return list(results)


def halves(x):
    high = x.astype(BF16)
    return high, (x - high.astype(F32)).astype(BF16)


def paired(x):
    return jnp.concatenate(halves(x), axis=1)


def dot(a, b):
    return jnp.dot(a, b, preferred_element_type=F32)


def dot_first(a, b):
    return lax.dot_general(a, b, (((0,), (0,)), ((), ())), preferred_element_type=F32)


def folded(x):
    columns = x.shape[1] // 2
    return x[:, :columns] + x[:, columns:]


def blocks(order, count=4):
    rows = order // count
    return [pl.ds(index * rows, rows) for index in range(count)]


def put_pair(out, at, x):
    columns = x.shape[1]
    out[at, :columns], out[at, columns:] = halves(x)


def arrived(flags, block, received):
    return jnp.where(flags[0, 4 + block] > 0.5, received[block][...], 0.0)


def numbers_kernel(spectrum, numbers, place):
    groups, subs = lax.axis_size("grp"), lax.axis_size("sub")
    grp, sub = lax.axis_index("grp"), lax.axis_index("sub")
    lanes = lax.broadcasted_iota(jnp.int32, (1, 128), 1)

    def lined(values, zero):
        out = jnp.full((1, 128), zero)
        for index, value in enumerate(values):
            out = jnp.where(lanes == index, value, out)
        return out

    low, high = jnp.full((1, 128), spectrum[0]), jnp.full((1, 128), spectrum[1])
    centre, half_width = 0.5 * (low + high), 0.5 * (high - low)
    rho = half_width / centre
    factors = [0.0, 1.0 / centre]
    for _ in range(ITERS - 1):
        rho_next = 1.0 / (2.0 * centre / half_width - rho)
        factors += [rho_next * rho, 2.0 * rho_next / half_width]
        rho = rho_next
    odd_core, odd_group = (sub & 1) == 1, (grp & 1) == 1
    none = [
        sub == jnp.where(odd_core, subs - 1, 0),
        grp == jnp.where(odd_group, groups - 1, 0),
        grp == jnp.where(odd_group, 0, groups - 1),
        sub == jnp.where(odd_core, 0, subs - 1),
    ]
    weights = [jnp.where(x, 1.0, 0.5) for x in none]
    has = [jnp.where(x, 0.0, 1.0) for x in none]
    numbers[...] = lined(weights + has + factors, 0.0)
    place[...] = lined([sub >> 3, (sub >> 1) & 3, grp & 3, grp >> 2, grp, sub & 1], 0)


def load_kernel(load, place, to_faces, f0, f1, f2, f3, parts):
    order, rows = load.shape[0], 144

    @pl.loop(0, order // rows)
    def _(step):
        at = pl.ds(pl.multiple_of(step * rows, rows), rows)
        lanes = lax.broadcasted_iota(jnp.int32, (rows, order), 1)
        to_faces[at, :] = jnp.where(place[at, :] == lanes, 1.0, 0.0).astype(BF16)

    put_pair(parts, slice(None), load[...])
    for at, out in zip(blocks(order), (f0, f1, f2, f3)):
        out[...] = folded(dot(to_faces[at, :], parts[...]))


def basis_kernel(basis, modes, to_local, to_faces, rows, columns):
    both_parts = jnp.concatenate(halves(basis[...]), axis=0)
    top = lax.dot_general(
        modes[...], basis[...], (((0,), (0,)), ((), ())), precision=EXACT, preferred_element_type=F32
    )
    all_parts = jnp.concatenate([both_parts, *halves(top)], axis=0)
    rows[...] = dot(all_parts, to_local[...]).astype(BF16)
    columns[...] = lax.dot_general(
        to_faces[...], both_parts, (((1,), (1,)), ((), ())), preferred_element_type=F32
    ).astype(BF16)


def split_kernel(matrix, after, high, low):
    del after
    rows = 144

    @pl.loop(0, matrix.shape[0] // rows)
    def _(step):
        at = pl.ds(pl.multiple_of(step * rows, rows), rows)
        high[at, :], low[at, :] = halves(matrix[at, :])


def onehot_kernel(place, to_local):
    order, rows = place.shape[1], 144

    @pl.loop(0, order // rows)
    def _(step):
        at = pl.ds(pl.multiple_of(step * rows, rows), rows)
        row = lax.broadcasted_iota(jnp.int32, (rows, order), 0) + step * rows
        to_local[at, :] = jnp.where(place[...] == row, 1.0, 0.0).astype(BF16)


def residual_kernel(first, *refs):
    refs = list(refs)
    flags, basis = refs[:2]
    del refs[:2]
    before = None if first else refs.pop(0)
    own, received = refs[:4], refs[4:8]
    residual, parts, coarse_top = refs[8:]
    order = residual.shape[0]
    for block, at in enumerate(blocks(order)):
        total = own[block][...] + arrived(flags, block, received)
        if not first:
            total = before[at, :] - total
        residual[at, :] = total
        put_pair(parts, at, total * flags[0, block])
    product = folded(dot(basis[...], parts[...]))
    count = product.shape[0] // 4
    coarse_top[:count, :] = product[:count, :] + product[count : 2 * count, :]
    coarse_top[count:, :] = product[2 * count : 3 * count, :] + product[3 * count :, :]


def apply(high, low, to_local, to_faces, parts, vectors, results, outs):
    order = parts.shape[0]
    for at in blocks(order):
        vectors[at, :] = dot(to_local[at, :], parts[...]).astype(BF16)
    for at in blocks(order):
        product = folded(dot(high[at, :], vectors[...]) + dot(low[at, :], vectors[...]))
        put_pair(results, at, product)
    for at, out in zip(blocks(order), outs):
        out[...] = folded(dot(to_faces[at, :], results[...]))


def product_kernel(high, low, to_local, to_faces, parts, o0, o1, o2, o3, vectors, results):
    apply(high, low, to_local, to_faces, parts, vectors, results, (o0, o1, o2, o3))


def level_kernel(count, own, one, two, three, out):
    parts = (own, one, two, three)
    size = own.shape[0] - count
    for index, part in enumerate(parts):
        out[index * size : (index + 1) * size, :] = part[:size, :]
    out[4 * size :, :] = (own[size:, :] + one[size:, :]) + (two[size:, :] + three[size:, :])


def total_kernel(own, other, out):
    count = out.shape[0]
    at = pl.ds(own.shape[0] - count, count)
    out[...] = own[at, :] + other[at, :]


def group_kernel(place, inverse, own, other, out, vectors):
    high_row, row, core = place[0, 0], place[0, 1], place[0, 5]
    width, columns = out.shape
    for by_core, part in enumerate((own, other)):
        for by_row in range(4):
            for by_high in range(4):
                flips = by_core ^ (by_row > 0) ^ (by_high > 0)
                spot = ((high_row ^ by_high) * 4 + (row ^ by_row)) * 2 + (core ^ int(flips))
                at = pl.ds(pl.multiple_of(spot * width, width), width)
                source = (by_row * 4 + by_high) * width
                put_pair(vectors, at, part[source : source + width, :])
    product = folded(dot(jnp.concatenate(halves(inverse[...]), axis=0), vectors[...]))
    out[...] = product[:width, :] + product[width:, :]


def small_dot(a, b):
    product = folded(dot(jnp.concatenate(halves(a), axis=0), paired(b)))
    count = a.shape[0]
    return product[:count, :] + product[count:, :]


def apex_rows(place, top, index, count):
    rows = top[pl.ds(pl.multiple_of(index * count, count), count), :]
    span = rows.shape[1] // 2
    return jnp.where(place[0, 3] == 0, rows[:, :span], rows[:, span:])


def apex_kernel(place, top, own, one, two, three, other, ordered):
    count = own.shape[0]
    for by_column, part in enumerate((own, one, two, three)):
        spot = place[0, 2] ^ by_column
        ordered[pl.ds(pl.multiple_of(spot * count, count), count), :] = part[...]
    rows = apex_rows(place, top, place[0, 4] ^ 4, count)
    other[...] = small_dot(rows, ordered[...])


def partial_kernel(place, top, modes, ordered, grouped, out):
    rows = apex_rows(place, top, place[0, 4], grouped.shape[0])
    out[...] = grouped[...] + small_dot(modes[...], small_dot(rows, ordered[...]))


def prolong_kernel(flags, basis, modes, partial, theirs, l0, l1, l2, l3, f0, f1, f2, f3):
    correction = partial[...] + small_dot(modes[...], theirs[...])
    vectors = paired(correction)
    vectors = jnp.concatenate([vectors, vectors], axis=0)
    sources, outs = (l0, l1, l2, l3), (f0, f1, f2, f3)
    for block, at in enumerate(blocks(basis.shape[0])):
        lifted = folded(dot(basis[at, :], vectors))
        outs[block][...] = (sources[block][...] + lifted) * flags[0, block]


def direction_kernel(step, *refs):
    refs, first = list(refs), step == 0
    flags, high, low, to_local, to_faces = refs[:5]
    del refs[:5]
    old, new = flags[0, 8 + 2 * step], flags[0, 9 + 2 * step]
    before, solved = (None, None) if first else (refs.pop(0), refs.pop(0))
    own, received = refs[:4], refs[4:8]
    direction, solution_out = refs[8:10]
    faces, (parts, vectors) = refs[10:14], refs[14:]
    order = direction.shape[0]
    for block, at in enumerate(blocks(order)):
        total = (own[block][...] + arrived(flags, block, received)) * new
        if not first:
            total = old * before[at, :] + total
        direction[at, :] = total
        solution_out[at, :] = total if first else solved[at, :] + total
        put_pair(parts, at, total)
    apply(high, low, to_local, to_faces, parts, vectors, parts, faces)


def local_kernel(to_local, values, out, parts):
    put_pair(parts, slice(None), values[...])
    for at in blocks(out.shape[0]):
        out[at, :] = folded(dot(to_local[at, :], parts[...]))


def last_kernel(flags, to_local, before, *refs):
    own, received, (out, whole, parts) = refs[:4], refs[4:8], refs[8:]
    for block, at in enumerate(blocks(out.shape[0])):
        whole[at, :] = before[at, :] - (own[block][...] + arrived(flags, block, received))
    local_kernel(to_local, whole, out, parts)


def both(pairs):
    return pairs + [(b, a) for a, b in pairs]


def shards(
    load_cases,
    schur_matrix,
    local_inverse,
    coarse_basis,
    group_inverse,
    group_modes,
    top_inverse,
    face_map,
    spectrum,
):
    order, columns = load_cases.shape
    modes = coarse_basis.shape[0]
    face = order // 4
    groups, subs = lax.axis_size("grp"), lax.axis_size("sub")
    grp, sub = lax.axis_index("grp"), lax.axis_index("sub")
    odd_core = (sub & 1) == 1
    odd_group = (grp & 1) == 1

    by_face = face_map.reshape(4, face)
    order_of = jnp.stack(
        [
            jnp.where(odd_core, by_face[3], by_face[2]),
            jnp.where(odd_group, by_face[1], by_face[0]),
            jnp.where(odd_group, by_face[0], by_face[1]),
            jnp.where(odd_core, by_face[2], by_face[3]),
        ]
    )
    place_row, place_column = order_of.reshape(1, order), order_of.reshape(order, 1)
    numbers, place = call(
        numbers_kernel, [((1, 128), F32), ((1, 128), jnp.int32)], [("s", spectrum)]
    )

    place_row, place_column = lax.optimization_barrier((place_row, place_column))

    routes = (
        ("sub", both([(i, (i + 1) % subs) for i in range(1, subs, 2)])),
        ("grp", both([(i, (i + 1) % groups) for i in range(1, groups, 2)])),
        ("grp", both([(i, i + 1) for i in range(0, groups, 2)])),
        ("sub", both([(i, i + 1) for i in range(0, subs, 2)])),
    )

    def exchange(faces):
        return [lax.ppermute(part, *route) for part, route in zip(faces, routes)]

    def across_sub(x, mask):
        return lax.ppermute(x, "sub", [(i, i ^ mask ^ 1) for i in range(subs)])

    def across_grp(x, mask):
        pairs = [
            (g * subs + i, (g ^ mask) * subs + (i ^ 1)) for g in range(groups) for i in range(subs)
        ]
        return lax.ppermute(x, ("grp", "sub"), pairs)

    def across_core(x):
        return lax.ppermute(x, "sub", [(i, i ^ 1) for i in range(subs)])

    block = ((face, columns), F32)
    field = ((order, columns), F32)
    square = ((order, order), BF16)
    pair = pltpu.VMEM((order, 2 * columns), BF16)

    to_faces, *faces = call(
        load_kernel,
        [square] + [block] * 4,
        [("v", load_cases), ("v", place_column)],
        [pair],
        LARGE,
    )
    received = exchange(faces)
    (to_local,) = call(onehot_kernel, [square], [("v", place_row)])
    basis_rows, basis_columns = call(
        basis_kernel,
        [((4 * modes, order), BF16), ((order, 2 * modes), BF16)],
        [("v", x) for x in (coarse_basis, group_modes, to_local, to_faces)],
        limit=LARGE,
    )
    matrices = {}

    def split(name, matrix, after):
        if name not in matrices:
            matrices[name] = call(split_kernel, [square] * 2, [("v", matrix), ("a", after)])
        return matrices[name]

    def update(residual, faces, received):
        first = residual is None
        ins = [("s", numbers), ("v", basis_rows)]
        ins += ([] if first else [("v", residual)]) + [("v", x) for x in faces + received]
        return call(
            functools.partial(residual_kernel, first),
            [field, ((order, 2 * columns), BF16), ((2 * modes, columns), F32)],
            ins,
            limit=LARGE,
        )

    def precondition(step, weighted, coarse_top):
        def product():
            return call(
                product_kernel,
                [block] * 4,
                [("v", x) for x in (*inverse, to_local, to_faces, weighted)],
                [pair] * 2,
                LARGE,
                flops=1 << 30,
            )

        inverse = split("inverse", local_inverse, coarse_top)
        others = [across_sub(coarse_top, mask) for mask in (8, 16, 24)]
        if step == 0:
            others, inverse = lax.optimization_barrier((others, inverse))
        else:
            others, local_part = lax.optimization_barrier((others, product()))
        (level,) = call(
            functools.partial(level_kernel, modes),
            [((5 * modes, columns), F32)],
            [("v", x) for x in [coarse_top] + others],
        )
        others = [across_sub(level, mask) for mask in (2, 4, 6)]
        if step == 0:
            others, local_part = lax.optimization_barrier((others, product()))
        (level,) = call(
            functools.partial(level_kernel, modes),
            [((17 * modes, columns), F32)],
            [("v", x) for x in [level] + others],
        )
        gathered = [("v", level), ("v", across_core(level))]
        (top_term,) = call(total_kernel, [((modes, columns), F32)], gathered)
        (grouped,) = call(
            group_kernel,
            [((modes, columns), F32)],
            [("s", place), ("v", group_inverse)] + gathered,
            [pltpu.VMEM((group_inverse.shape[1], 2 * columns), BF16)],
            flops=1 << 26,
        )
        others = [across_grp(top_term, mask) for mask in (1, 2, 3)]
        if step == 0:
            schur = split("schur", schur_matrix, top_term)
            others, matrices["schur"] = lax.optimization_barrier((others, schur))
        others, grouped = lax.optimization_barrier((others, grouped))
        other, ordered = call(
            apex_kernel,
            [((modes, columns), F32), ((4 * modes, columns), F32)],
            [("s", place), ("v", top_inverse)] + [("v", x) for x in [top_term] + others],
        )
        theirs = across_grp(other, 4)
        (partial,) = call(
            partial_kernel,
            [((modes, columns), F32)],
            [("s", place)] + [("v", x) for x in (top_inverse, group_modes, ordered, grouped)],
        )
        theirs, partial = lax.optimization_barrier((theirs, partial))
        ins = [basis_columns, group_modes, partial, theirs] + local_part
        return call(
            prolong_kernel,
            [block] * 4,
            [("s", numbers)] + [("v", x) for x in ins],
            limit=LARGE,
        )

    residual = direction = solved = None
    for step in range(ITERS):
        residual, weighted, coarse_top = update(residual, faces, received)
        faces = precondition(step, weighted, coarse_top)
        received = exchange(faces)
        ins = [("s", numbers)]
        ins += [("v", x) for x in (*matrices["schur"], to_local, to_faces)]
        ins += [] if step == 0 else [("v", direction), ("v", solved)]
        direction, solved, *faces = call(
            functools.partial(direction_kernel, step),
            [field, field] + [block] * 4,
            ins + [("v", x) for x in faces + received],
            [pair] * 2,
            LARGE,
            flops=1 << 30,
        )
        received = exchange(faces)
    (displacement,) = call(
        local_kernel, [field], [("v", to_local), ("v", solved)], [pair], LARGE, flops=1 << 28
    )
    (remainder,) = call(
        last_kernel,
        [field],
        [("s", numbers), ("v", to_local), ("v", residual)] + [("v", x) for x in faces + received],
        [pltpu.VMEM((order, columns), F32), pair],
        LARGE,
    )
    return displacement, remainder


def solution(mesh):
    placed = (
        P(("grp", "sub"), None),
        P(("grp", "sub"), None),
        P(("grp", "sub"), None),
        P(("grp", "sub"), None),
        P(("grp", "sub"), None),
        P(("grp", "sub"), None),
        P(),
        P(("grp", "sub"), None),
        P(),
    )
    return jax.shard_map(
        shards,
        mesh=mesh,
        in_specs=placed,
        out_specs=(P(("grp", "sub"), None), P(("grp", "sub"), None)),
        check_vma=False,
    )
```

```python
import functools

import jax
import jax.numpy as jnp
from jax import lax
from jax.experimental import pallas as pl
from jax.experimental.pallas import tpu as pltpu
from jax.sharding import PartitionSpec as P

ITERS = 3
F32, BF16 = jnp.float32, jnp.bfloat16
EXACT = lax.Precision.HIGHEST
VMEM = pl.BlockSpec(memory_space=pltpu.VMEM)
SMEM = pl.BlockSpec(memory_space=pltpu.SMEM)
LARGE = 8 << 20


def call(kernel, outs, ins, scratch=(), limit=2 << 20, flops=1 << 20):
    spaces = {"s": SMEM, "v": VMEM, "a": pl.BlockSpec(memory_space=pl.ANY)}
    specs = [spaces[kind] for kind, _ in ins]
    results = pl.pallas_call(
        kernel,
        out_shape=[jax.ShapeDtypeStruct(shape, dtype) for shape, dtype in outs],
        in_specs=specs,
        out_specs=[VMEM] * len(outs),
        scratch_shapes=list(scratch),
        compiler_params=pltpu.CompilerParams(vmem_limit_bytes=limit),
        cost_estimate=pl.CostEstimate(flops=flops, bytes_accessed=1 << 20, transcendentals=0),
    )(*[array for _, array in ins])
    return list(results)


def halves(x):
    high = x.astype(BF16)
    return high, (x - high.astype(F32)).astype(BF16)


def paired(x):
    return jnp.concatenate(halves(x), axis=1)


def dot(a, b):
    return jnp.dot(a, b, preferred_element_type=F32)


def dot_first(a, b):
    return lax.dot_general(a, b, (((0,), (0,)), ((), ())), preferred_element_type=F32)


def folded(x):
    columns = x.shape[1] // 2
    return x[:, :columns] + x[:, columns:]


def blocks(order, count=4):
    rows = order // count
    return [pl.ds(index * rows, rows) for index in range(count)]


def put_pair(out, at, x):
    columns = x.shape[1]
    out[at, :columns], out[at, columns:] = halves(x)


def arrived(flags, block, received):
    return jnp.where(flags[0, 4 + block] > 0.5, received[block][...], 0.0)


def numbers_kernel(spectrum, numbers, place):
    groups, subs = lax.axis_size("grp"), lax.axis_size("sub")
    grp, sub = lax.axis_index("grp"), lax.axis_index("sub")
    lanes = lax.broadcasted_iota(jnp.int32, (1, 128), 1)

    def lined(values, zero):
        out = jnp.full((1, 128), zero)
        for index, value in enumerate(values):
            out = jnp.where(lanes == index, value, out)
        return out

    low, high = jnp.full((1, 128), spectrum[0]), jnp.full((1, 128), spectrum[1])
    centre, half_width = 0.5 * (low + high), 0.5 * (high - low)
    rho = half_width / centre
    factors = [0.0, 1.0 / centre]
    for _ in range(ITERS - 1):
        rho_next = 1.0 / (2.0 * centre / half_width - rho)
        factors += [rho_next * rho, 2.0 * rho_next / half_width]
        rho = rho_next
    odd_core, odd_group = (sub & 1) == 1, (grp & 1) == 1
    none = [
        sub == jnp.where(odd_core, subs - 1, 0),
        grp == jnp.where(odd_group, groups - 1, 0),
        grp == jnp.where(odd_group, 0, groups - 1),
        sub == jnp.where(odd_core, 0, subs - 1),
    ]
    weights = [jnp.where(x, 1.0, 0.5) for x in none]
    has = [jnp.where(x, 0.0, 1.0) for x in none]
    numbers[...] = lined(weights + has + factors, 0.0)
    place[...] = lined([sub >> 3, (sub >> 1) & 3, grp & 3, grp >> 2, grp, sub & 1], 0)


def load_kernel(load, place, to_faces, f0, f1, f2, f3, parts, held, arrival):
    order, rows = load.shape[0], 144
    copy = pltpu.make_async_copy(load, held, arrival)
    copy.start()

    @pl.loop(0, order // rows)
    def _(step):
        at = pl.ds(pl.multiple_of(step * rows, rows), rows)
        lanes = lax.broadcasted_iota(jnp.int32, (rows, order), 1)
        to_faces[at, :] = jnp.where(place[at, :] == lanes, 1.0, 0.0).astype(BF16)

    copy.wait()
    put_pair(parts, slice(None), held[...])
    for at, out in zip(blocks(order), (f0, f1, f2, f3)):
        out[...] = folded(dot(to_faces[at, :], parts[...]))


def basis_kernel(basis, modes, to_local, to_faces, rows, columns):
    both_parts = jnp.concatenate(halves(basis[...]), axis=0)
    top = lax.dot_general(
        modes[...], basis[...], (((0,), (0,)), ((), ())), precision=EXACT, preferred_element_type=F32
    )
    all_parts = jnp.concatenate([both_parts, *halves(top)], axis=0)
    rows[...] = dot(all_parts, to_local[...]).astype(BF16)
    columns[...] = lax.dot_general(
        to_faces[...], both_parts, (((1,), (1,)), ((), ())), preferred_element_type=F32
    ).astype(BF16)


def split_kernel(matrix, after, high, low):
    del after
    rows = 144

    @pl.loop(0, matrix.shape[0] // rows)
    def _(step):
        at = pl.ds(pl.multiple_of(step * rows, rows), rows)
        high[at, :], low[at, :] = halves(matrix[at, :])


def columns_kernel(part, matrix, to_local, after, out):
    del after
    for at in blocks(matrix.shape[0]):
        out[at, :] = dot(halves(matrix[at, :])[part], to_local[...]).astype(BF16)


def onehot_kernel(place, to_local):
    order, rows = place.shape[1], 144

    @pl.loop(0, order // rows)
    def _(step):
        at = pl.ds(pl.multiple_of(step * rows, rows), rows)
        row = lax.broadcasted_iota(jnp.int32, (rows, order), 0) + step * rows
        to_local[at, :] = jnp.where(place[...] == row, 1.0, 0.0).astype(BF16)


def residual_kernel(first, *refs):
    refs = list(refs)
    flags, basis = refs[:2]
    del refs[:2]
    before = None if first else refs.pop(0)
    own, received = refs[:4], refs[4:8]
    residual, parts, coarse_top = refs[8:]
    order = residual.shape[0]
    for block, at in enumerate(blocks(order)):
        total = own[block][...] + arrived(flags, block, received)
        if not first:
            total = before[at, :] - total
        residual[at, :] = total
        put_pair(parts, at, total * flags[0, block])
    product = folded(dot(basis[...], parts[...]))
    count = product.shape[0] // 4
    coarse_top[:count, :] = product[:count, :] + product[count : 2 * count, :]
    coarse_top[count:, :] = product[2 * count : 3 * count, :] + product[3 * count :, :]


def apply(high, low, to_faces, vectors, results, outs):
    order = vectors.shape[0]
    for at in blocks(order):
        product = folded(dot(high[at, :], vectors[...]) + dot(low[at, :], vectors[...]))
        put_pair(results, at, product)
    for at, out in zip(blocks(order), outs):
        out[...] = folded(dot(to_faces[at, :], results[...]))


def product_kernel(high, low, to_local, to_faces, parts, o0, o1, o2, o3, vectors, results):
    for at in blocks(parts.shape[0]):
        vectors[at, :] = dot(to_local[at, :], parts[...]).astype(BF16)
    apply(high, low, to_faces, vectors, results, (o0, o1, o2, o3))


def level_kernel(count, own, one, two, three, out):
    parts = (own, one, two, three)
    size = own.shape[0] - count
    for index, part in enumerate(parts):
        out[index * size : (index + 1) * size, :] = part[:size, :]
    out[4 * size :, :] = (own[size:, :] + one[size:, :]) + (two[size:, :] + three[size:, :])


def total_kernel(own, other, out):
    count = out.shape[0]
    at = pl.ds(own.shape[0] - count, count)
    out[...] = own[at, :] + other[at, :]


def group_kernel(place, inverse, own, other, out, vectors):
    high_row, row, core = place[0, 0], place[0, 1], place[0, 5]
    width, columns = out.shape
    for by_core, part in enumerate((own, other)):
        for by_row in range(4):
            for by_high in range(4):
                flips = by_core ^ (by_row > 0) ^ (by_high > 0)
                spot = ((high_row ^ by_high) * 4 + (row ^ by_row)) * 2 + (core ^ int(flips))
                at = pl.ds(pl.multiple_of(spot * width, width), width)
                source = (by_row * 4 + by_high) * width
                put_pair(vectors, at, part[source : source + width, :])
    product = folded(dot(jnp.concatenate(halves(inverse[...]), axis=0), vectors[...]))
    out[...] = product[:width, :] + product[width:, :]


def small_dot(a, b):
    product = folded(dot(jnp.concatenate(halves(a), axis=0), paired(b)))
    count = a.shape[0]
    return product[:count, :] + product[count:, :]


def apex_rows(place, top, index, count):
    rows = top[pl.ds(pl.multiple_of(index * count, count), count), :]
    span = rows.shape[1] // 2
    return jnp.where(place[0, 3] == 0, rows[:, :span], rows[:, span:])


def apex_kernel(place, top, own, one, two, three, other, ordered):
    count = own.shape[0]
    for by_column, part in enumerate((own, one, two, three)):
        spot = place[0, 2] ^ by_column
        ordered[pl.ds(pl.multiple_of(spot * count, count), count), :] = part[...]
    rows = apex_rows(place, top, place[0, 4] ^ 4, count)
    other[...] = small_dot(rows, ordered[...])


def partial_kernel(place, top, modes, ordered, grouped, out):
    rows = apex_rows(place, top, place[0, 4], grouped.shape[0])
    out[...] = grouped[...] + small_dot(modes[...], small_dot(rows, ordered[...]))


def prolong_kernel(flags, basis, modes, partial, theirs, l0, l1, l2, l3, f0, f1, f2, f3):
    correction = partial[...] + small_dot(modes[...], theirs[...])
    vectors = paired(correction)
    vectors = jnp.concatenate([vectors, vectors], axis=0)
    sources, outs = (l0, l1, l2, l3), (f0, f1, f2, f3)
    for block, at in enumerate(blocks(basis.shape[0])):
        lifted = folded(dot(basis[at, :], vectors))
        outs[block][...] = (sources[block][...] + lifted) * flags[0, block]


def direction_kernel(step, *refs):
    refs, first = list(refs), step == 0
    flags, high, low, to_faces = refs[:4]
    del refs[:4]
    old, new = flags[0, 8 + 2 * step], flags[0, 9 + 2 * step]
    before, solved = (None, None) if first else (refs.pop(0), refs.pop(0))
    own, received = refs[:4], refs[4:8]
    direction, solution_out = refs[8:10]
    faces, (parts, results) = refs[10:14], refs[14:]
    order = direction.shape[0]
    for block, at in enumerate(blocks(order)):
        total = (own[block][...] + arrived(flags, block, received)) * new
        if not first:
            total = old * before[at, :] + total
        direction[at, :] = total
        solution_out[at, :] = total if first else solved[at, :] + total
        put_pair(parts, at, total)
    apply(high, low, to_faces, parts, results, faces)


def local_kernel(to_local, values, out, parts):
    put_pair(parts, slice(None), values[...])
    for at in blocks(out.shape[0]):
        out[at, :] = folded(dot(to_local[at, :], parts[...]))


def last_kernel(flags, to_local, before, *refs):
    own, received, (out, whole, parts) = refs[:4], refs[4:8], refs[8:]
    for block, at in enumerate(blocks(out.shape[0])):
        whole[at, :] = before[at, :] - (own[block][...] + arrived(flags, block, received))
    local_kernel(to_local, whole, out, parts)


def both(pairs):
    return pairs + [(b, a) for a, b in pairs]


def shards(
    load_cases,
    schur_matrix,
    local_inverse,
    coarse_basis,
    group_inverse,
    group_modes,
    top_inverse,
    face_map,
    spectrum,
):
    order, columns = load_cases.shape
    modes = coarse_basis.shape[0]
    face = order // 4
    groups, subs = lax.axis_size("grp"), lax.axis_size("sub")
    grp, sub = lax.axis_index("grp"), lax.axis_index("sub")
    odd_core = (sub & 1) == 1
    odd_group = (grp & 1) == 1

    by_face = face_map.reshape(4, face)
    order_of = jnp.stack(
        [
            jnp.where(odd_core, by_face[3], by_face[2]),
            jnp.where(odd_group, by_face[1], by_face[0]),
            jnp.where(odd_group, by_face[0], by_face[1]),
            jnp.where(odd_core, by_face[2], by_face[3]),
        ]
    )
    place_row, place_column = order_of.reshape(1, order), order_of.reshape(order, 1)
    numbers, place = call(
        numbers_kernel, [((1, 128), F32), ((1, 128), jnp.int32)], [("s", spectrum)]
    )

    place_row, place_column = lax.optimization_barrier((place_row, place_column))

    routes = (
        ("sub", both([(i, (i + 1) % subs) for i in range(1, subs, 2)])),
        ("grp", both([(i, (i + 1) % groups) for i in range(1, groups, 2)])),
        ("grp", both([(i, i + 1) for i in range(0, groups, 2)])),
        ("sub", both([(i, i + 1) for i in range(0, subs, 2)])),
    )

    def exchange(faces):
        return [lax.ppermute(part, *route) for part, route in zip(faces, routes)]

    def across_sub(x, mask):
        return lax.ppermute(x, "sub", [(i, i ^ mask ^ 1) for i in range(subs)])

    def across_grp(x, mask):
        pairs = [
            (g * subs + i, (g ^ mask) * subs + (i ^ 1)) for g in range(groups) for i in range(subs)
        ]
        return lax.ppermute(x, ("grp", "sub"), pairs)

    def across_core(x):
        return lax.ppermute(x, "sub", [(i, i ^ 1) for i in range(subs)])

    block = ((face, columns), F32)
    field = ((order, columns), F32)
    square = ((order, order), BF16)
    pair = pltpu.VMEM((order, 2 * columns), BF16)

    to_faces, *faces = call(
        load_kernel,
        [square] + [block] * 4,
        [("a", load_cases), ("v", place_column)],
        [pair, pltpu.VMEM((order, columns), F32), pltpu.SemaphoreType.DMA],
        LARGE,
    )
    received = exchange(faces)
    (to_local,) = call(onehot_kernel, [square], [("v", place_row)])
    basis_rows, basis_columns = call(
        basis_kernel,
        [((4 * modes, order), BF16), ((order, 2 * modes), BF16)],
        [("v", x) for x in (coarse_basis, group_modes, to_local, to_faces)],
        limit=LARGE,
    )
    inverse = call(split_kernel, [square] * 2, [("v", local_inverse), ("a", basis_rows)])
    received, inverse = lax.optimization_barrier((received, inverse))
    schur = [None, None]

    def schur_part(part, after):
        ins = [("v", schur_matrix), ("v", to_local), ("a", after)]
        kernel = functools.partial(columns_kernel, part)
        return call(kernel, [square], ins, limit=LARGE, flops=1 << 31)[0]

    def update(residual, faces, received):
        first = residual is None
        ins = [("s", numbers), ("v", basis_rows)]
        ins += ([] if first else [("v", residual)]) + [("v", x) for x in faces + received]
        return call(
            functools.partial(residual_kernel, first),
            [field, ((order, 2 * columns), BF16), ((2 * modes, columns), F32)],
            ins,
            limit=LARGE,
        )

    def precondition(step, weighted, coarse_top):
        def product():
            return call(
                product_kernel,
                [block] * 4,
                [("v", x) for x in (*inverse, to_local, to_faces, weighted)],
                [pair] * 2,
                LARGE,
                flops=1 << 30,
            )

        others = [across_sub(coarse_top, mask) for mask in (8, 24, 16)]
        if step == 0:
            others, schur[0] = lax.optimization_barrier((others, schur_part(0, coarse_top)))
        (level,) = call(
            functools.partial(level_kernel, modes),
            [((5 * modes, columns), F32)],
            [("v", x) for x in (coarse_top, others[0], others[2], others[1])],
        )
        others = [across_sub(level, mask) for mask in (2, 6, 4)]
        others, local_part = lax.optimization_barrier((others, product()))
        (level,) = call(
            functools.partial(level_kernel, modes),
            [((17 * modes, columns), F32)],
            [("v", x) for x in (level, others[0], others[2], others[1])],
        )
        gathered = [("v", level), ("v", across_core(level))]
        (top_term,) = call(total_kernel, [((modes, columns), F32)], gathered)
        (grouped,) = call(
            group_kernel,
            [((modes, columns), F32)],
            [("s", place), ("v", group_inverse)] + gathered,
            [pltpu.VMEM((group_inverse.shape[1], 2 * columns), BF16)],
            flops=1 << 26,
        )
        others = [across_grp(top_term, mask) for mask in (1, 3, 2)]
        others, grouped = lax.optimization_barrier((others, grouped))
        other, ordered = call(
            apex_kernel,
            [((modes, columns), F32), ((4 * modes, columns), F32)],
            [("s", place), ("v", top_inverse)] + [("v", x) for x in (top_term, others[0], others[2], others[1])],
        )
        theirs = across_grp(other, 4)
        (partial,) = call(
            partial_kernel,
            [((modes, columns), F32)],
            [("s", place)] + [("v", x) for x in (top_inverse, group_modes, ordered, grouped)],
        )
        theirs, partial = lax.optimization_barrier((theirs, partial))
        ins = [basis_columns, group_modes, partial, theirs] + local_part
        return call(
            prolong_kernel,
            [block] * 4,
            [("s", numbers)] + [("v", x) for x in ins],
            limit=LARGE,
        )

    residual = direction = solved = None
    for step in range(ITERS):
        residual, weighted, coarse_top = update(residual, faces, received)
        faces = precondition(step, weighted, coarse_top)
        received = exchange(faces)
        if step == 0:
            received, schur[1] = lax.optimization_barrier((received, schur_part(1, faces[3])))
        ins = [("s", numbers)]
        ins += [("v", x) for x in (*schur, to_faces)]
        ins += [] if step == 0 else [("v", direction), ("v", solved)]
        direction, solved, *faces = call(
            functools.partial(direction_kernel, step),
            [field, field] + [block] * 4,
            ins + [("v", x) for x in faces + received],
            [pair] * 2,
            LARGE,
            flops=1 << 30,
        )
        received = exchange(faces)
    (displacement,) = call(
        local_kernel, [field], [("v", to_local), ("v", solved)], [pair], LARGE, flops=1 << 28
    )
    (remainder,) = call(
        last_kernel,
        [field],
        [("s", numbers), ("v", to_local), ("v", residual)] + [("v", x) for x in faces + received],
        [pltpu.VMEM((order, columns), F32), pair],
        LARGE,
    )
    return displacement, remainder


def solution(mesh):
    placed = (
        P(("grp", "sub"), None),
        P(("grp", "sub"), None),
        P(("grp", "sub"), None),
        P(("grp", "sub"), None),
        P(("grp", "sub"), None),
        P(("grp", "sub"), None),
        P(),
        P(("grp", "sub"), None),
        P(),
    )
    return jax.shard_map(
        shards,
        mesh=mesh,
        in_specs=placed,
        out_specs=(P(("grp", "sub"), None), P(("grp", "sub"), None)),
        check_vma=False,
    )
```

```python
import functools

import jax
import jax.numpy as jnp
from jax import lax
from jax.experimental import pallas as pl
from jax.experimental.pallas import tpu as pltpu
from jax.sharding import PartitionSpec as P

ITERS = 3
F32, BF16 = jnp.float32, jnp.bfloat16
EXACT = lax.Precision.HIGHEST
VMEM = pl.BlockSpec(memory_space=pltpu.VMEM)
SMEM = pl.BlockSpec(memory_space=pltpu.SMEM)
LARGE = 8 << 20


def call(kernel, outs, ins, scratch=(), limit=2 << 20, flops=1 << 20):
    spaces = {"s": SMEM, "v": VMEM, "a": pl.BlockSpec(memory_space=pl.ANY)}
    specs = [spaces[kind] for kind, _ in ins]
    results = pl.pallas_call(
        kernel,
        out_shape=[jax.ShapeDtypeStruct(shape, dtype) for shape, dtype in outs],
        in_specs=specs,
        out_specs=[VMEM] * len(outs),
        scratch_shapes=list(scratch),
        compiler_params=pltpu.CompilerParams(vmem_limit_bytes=limit),
        cost_estimate=pl.CostEstimate(flops=flops, bytes_accessed=1 << 20, transcendentals=0),
    )(*[array for _, array in ins])
    return list(results)


def halves(x):
    high = x.astype(BF16)
    return high, (x - high.astype(F32)).astype(BF16)


def paired(x):
    return jnp.concatenate(halves(x), axis=1)


def dot(a, b):
    return jnp.dot(a, b, preferred_element_type=F32)


def dot_first(a, b):
    return lax.dot_general(a, b, (((0,), (0,)), ((), ())), preferred_element_type=F32)


def folded(x):
    columns = x.shape[1] // 2
    return x[:, :columns] + x[:, columns:]


def blocks(order, count=4):
    rows = order // count
    return [pl.ds(index * rows, rows) for index in range(count)]


def put_pair(out, at, x):
    columns = x.shape[1]
    out[at, :columns], out[at, columns:] = halves(x)


def arrived(flags, block, received):
    return jnp.where(flags[0, 4 + block] > 0.5, received[block][...], 0.0)


def numbers_kernel(spectrum, numbers, place):
    groups, subs = lax.axis_size("grp"), lax.axis_size("sub")
    grp, sub = lax.axis_index("grp"), lax.axis_index("sub")
    lanes = lax.broadcasted_iota(jnp.int32, (1, 128), 1)

    def lined(values, zero):
        out = jnp.full((1, 128), zero)
        for index, value in enumerate(values):
            out = jnp.where(lanes == index, value, out)
        return out

    low, high = jnp.full((1, 128), spectrum[0]), jnp.full((1, 128), spectrum[1])
    centre, half_width = 0.5 * (low + high), 0.5 * (high - low)
    rho = half_width / centre
    factors = [0.0, 1.0 / centre]
    for _ in range(ITERS - 1):
        rho_next = 1.0 / (2.0 * centre / half_width - rho)
        factors += [rho_next * rho, 2.0 * rho_next / half_width]
        rho = rho_next
    odd_core, odd_group = (sub & 1) == 1, (grp & 1) == 1
    none = [
        sub == jnp.where(odd_core, subs - 1, 0),
        grp == jnp.where(odd_group, groups - 1, 0),
        grp == jnp.where(odd_group, 0, groups - 1),
        sub == jnp.where(odd_core, 0, subs - 1),
    ]
    weights = [jnp.where(x, 1.0, 0.5) for x in none]
    has = [jnp.where(x, 0.0, 1.0) for x in none]
    numbers[...] = lined(weights + has + factors, 0.0)
    place[...] = lined([sub >> 3, (sub >> 1) & 3, grp & 3, grp >> 2, grp, sub & 1], 0)


def load_kernel(load, place, to_faces, f0, f1, f2, f3, parts, held, arrival):
    order, rows = load.shape[0], 144
    copy = pltpu.make_async_copy(load, held, arrival)
    copy.start()

    @pl.loop(0, order // rows)
    def _(step):
        at = pl.ds(pl.multiple_of(step * rows, rows), rows)
        lanes = lax.broadcasted_iota(jnp.int32, (rows, order), 1)
        to_faces[at, :] = jnp.where(place[at, :] == lanes, 1.0, 0.0).astype(BF16)

    copy.wait()
    put_pair(parts, slice(None), held[...])
    for at, out in zip(blocks(order), (f0, f1, f2, f3)):
        out[...] = folded(dot(to_faces[at, :], parts[...]))


def basis_kernel(basis, modes, to_local, to_faces, rows, columns):
    both_parts = jnp.concatenate(halves(basis[...]), axis=0)
    top = lax.dot_general(
        modes[...], basis[...], (((0,), (0,)), ((), ())), precision=EXACT, preferred_element_type=F32
    )
    all_parts = jnp.concatenate([both_parts, *halves(top)], axis=0)
    rows[...] = dot(all_parts, to_local[...]).astype(BF16)
    columns[...] = lax.dot_general(
        to_faces[...], both_parts, (((1,), (1,)), ((), ())), preferred_element_type=F32
    ).astype(BF16)


def split_kernel(matrix, after, high, low):
    del after
    rows = 144

    @pl.loop(0, matrix.shape[0] // rows)
    def _(step):
        at = pl.ds(pl.multiple_of(step * rows, rows), rows)
        high[at, :], low[at, :] = halves(matrix[at, :])


def columns_kernel(part, matrix, to_local, after, out):
    del after
    for at in blocks(matrix.shape[0]):
        out[at, :] = dot(halves(matrix[at, :])[part], to_local[...]).astype(BF16)


def rows_kernel(matrix, to_faces, after, out):
    del after
    for at in blocks(matrix.shape[0]):
        out[at, :] = dot(to_faces[at, :], matrix[...]).astype(BF16)


def onehot_kernel(place, to_local):
    order, rows = place.shape[1], 144

    @pl.loop(0, order // rows)
    def _(step):
        at = pl.ds(pl.multiple_of(step * rows, rows), rows)
        row = lax.broadcasted_iota(jnp.int32, (rows, order), 0) + step * rows
        to_local[at, :] = jnp.where(place[...] == row, 1.0, 0.0).astype(BF16)


def residual_kernel(first, *refs):
    refs = list(refs)
    flags, basis = refs[:2]
    del refs[:2]
    before = None if first else refs.pop(0)
    own, received = refs[:4], refs[4:8]
    residual, parts, coarse_top = refs[8:]
    order = residual.shape[0]
    for block, at in enumerate(blocks(order)):
        total = own[block][...] + arrived(flags, block, received)
        if not first:
            total = before[at, :] - total
        residual[at, :] = total
        put_pair(parts, at, total * flags[0, block])
    product = folded(dot(basis[...], parts[...]))
    count = product.shape[0] // 4
    coarse_top[:count, :] = product[:count, :] + product[count : 2 * count, :]
    coarse_top[count:, :] = product[2 * count : 3 * count, :] + product[3 * count :, :]


def apply(high, low, to_faces, vectors, results, outs):
    order = vectors.shape[0]
    for at in blocks(order):
        product = folded(dot(high[at, :], vectors[...]) + dot(low[at, :], vectors[...]))
        put_pair(results, at, product)
    for at, out in zip(blocks(order), outs):
        out[...] = folded(dot(to_faces[at, :], results[...]))


def product_kernel(high, low, to_local, to_faces, parts, o0, o1, o2, o3, vectors, results):
    for at in blocks(parts.shape[0]):
        vectors[at, :] = dot(to_local[at, :], parts[...]).astype(BF16)
    apply(high, low, to_faces, vectors, results, (o0, o1, o2, o3))


def level_kernel(count, own, one, two, three, out):
    parts = (own, one, two, three)
    size = own.shape[0] - count
    for index, part in enumerate(parts):
        out[index * size : (index + 1) * size, :] = part[:size, :]
    out[4 * size :, :] = (own[size:, :] + one[size:, :]) + (two[size:, :] + three[size:, :])


def total_kernel(own, other, out):
    count = out.shape[0]
    at = pl.ds(own.shape[0] - count, count)
    out[...] = own[at, :] + other[at, :]


def group_kernel(place, inverse, own, other, out, vectors):
    high_row, row, core = place[0, 0], place[0, 1], place[0, 5]
    width, columns = out.shape
    for by_core, part in enumerate((own, other)):
        for by_row in range(4):
            for by_high in range(4):
                flips = by_core ^ (by_row > 0) ^ (by_high > 0)
                spot = ((high_row ^ by_high) * 4 + (row ^ by_row)) * 2 + (core ^ int(flips))
                at = pl.ds(pl.multiple_of(spot * width, width), width)
                source = (by_row * 4 + by_high) * width
                put_pair(vectors, at, part[source : source + width, :])
    product = folded(dot(jnp.concatenate(halves(inverse[...]), axis=0), vectors[...]))
    out[...] = product[:width, :] + product[width:, :]


def small_dot(a, b):
    product = folded(dot(jnp.concatenate(halves(a), axis=0), paired(b)))
    count = a.shape[0]
    return product[:count, :] + product[count:, :]


def apex_rows(place, top, index, count):
    rows = top[pl.ds(pl.multiple_of(index * count, count), count), :]
    span = rows.shape[1] // 2
    return jnp.where(place[0, 3] == 0, rows[:, :span], rows[:, span:])


def apex_kernel(place, top, own, one, two, three, other, ordered):
    count = own.shape[0]
    for by_column, part in enumerate((own, one, two, three)):
        spot = place[0, 2] ^ by_column
        ordered[pl.ds(pl.multiple_of(spot * count, count), count), :] = part[...]
    rows = apex_rows(place, top, place[0, 4] ^ 4, count)
    other[...] = small_dot(rows, ordered[...])


def partial_kernel(place, top, modes, ordered, grouped, out):
    rows = apex_rows(place, top, place[0, 4], grouped.shape[0])
    out[...] = grouped[...] + small_dot(modes[...], small_dot(rows, ordered[...]))


def prolong_kernel(flags, basis, modes, partial, theirs, l0, l1, l2, l3, f0, f1, f2, f3):
    correction = partial[...] + small_dot(modes[...], theirs[...])
    vectors = paired(correction)
    vectors = jnp.concatenate([vectors, vectors], axis=0)
    sources, outs = (l0, l1, l2, l3), (f0, f1, f2, f3)
    for block, at in enumerate(blocks(basis.shape[0])):
        lifted = folded(dot(basis[at, :], vectors))
        outs[block][...] = (sources[block][...] + lifted) * flags[0, block]


def direction_kernel(step, *refs):
    refs, first = list(refs), step == 0
    flags, high, low = refs[:3]
    del refs[:3]
    to_faces = refs.pop(0) if first else None
    old, new = flags[0, 8 + 2 * step], flags[0, 9 + 2 * step]
    before, solved = (None, None) if first else (refs.pop(0), refs.pop(0))
    own, received = refs[:4], refs[4:8]
    direction, solution_out = refs[8:10]
    faces, parts = refs[10:14], refs[14]
    order = direction.shape[0]
    for block, at in enumerate(blocks(order)):
        total = (own[block][...] + arrived(flags, block, received)) * new
        if not first:
            total = old * before[at, :] + total
        direction[at, :] = total
        solution_out[at, :] = total if first else solved[at, :] + total
        put_pair(parts, at, total)
    if first:
        apply(high, low, to_faces, parts, refs[15], faces)
        return
    for at, out in zip(blocks(order), faces):
        out[...] = folded(dot(high[at, :], parts[...]) + dot(low[at, :], parts[...]))


def local_kernel(to_local, values, out, parts):
    put_pair(parts, slice(None), values[...])
    for at in blocks(out.shape[0]):
        out[at, :] = folded(dot(to_local[at, :], parts[...]))


def last_kernel(flags, to_local, before, *refs):
    own, received, (out, whole, parts) = refs[:4], refs[4:8], refs[8:]
    for block, at in enumerate(blocks(out.shape[0])):
        whole[at, :] = before[at, :] - (own[block][...] + arrived(flags, block, received))
    local_kernel(to_local, whole, out, parts)


def both(pairs):
    return pairs + [(b, a) for a, b in pairs]


def shards(
    load_cases,
    schur_matrix,
    local_inverse,
    coarse_basis,
    group_inverse,
    group_modes,
    top_inverse,
    face_map,
    spectrum,
):
    order, columns = load_cases.shape
    modes = coarse_basis.shape[0]
    face = order // 4
    groups, subs = lax.axis_size("grp"), lax.axis_size("sub")
    grp, sub = lax.axis_index("grp"), lax.axis_index("sub")
    odd_core = (sub & 1) == 1
    odd_group = (grp & 1) == 1

    by_face = face_map.reshape(4, face)
    order_of = jnp.stack(
        [
            jnp.where(odd_core, by_face[3], by_face[2]),
            jnp.where(odd_group, by_face[1], by_face[0]),
            jnp.where(odd_group, by_face[0], by_face[1]),
            jnp.where(odd_core, by_face[2], by_face[3]),
        ]
    )
    place_row, place_column = order_of.reshape(1, order), order_of.reshape(order, 1)
    numbers, place = call(
        numbers_kernel, [((1, 128), F32), ((1, 128), jnp.int32)], [("s", spectrum)]
    )

    place_row, place_column = lax.optimization_barrier((place_row, place_column))

    routes = (
        ("sub", both([(i, (i + 1) % subs) for i in range(1, subs, 2)])),
        ("grp", both([(i, (i + 1) % groups) for i in range(1, groups, 2)])),
        ("grp", both([(i, i + 1) for i in range(0, groups, 2)])),
        ("sub", both([(i, i + 1) for i in range(0, subs, 2)])),
    )

    def exchange(faces):
        return [lax.ppermute(part, *route) for part, route in zip(faces, routes)]

    def across_sub(x, mask):
        return lax.ppermute(x, "sub", [(i, i ^ mask ^ 1) for i in range(subs)])

    def across_grp(x, mask):
        pairs = [
            (g * subs + i, (g ^ mask) * subs + (i ^ 1)) for g in range(groups) for i in range(subs)
        ]
        return lax.ppermute(x, ("grp", "sub"), pairs)

    def across_core(x):
        return lax.ppermute(x, "sub", [(i, i ^ 1) for i in range(subs)])

    block = ((face, columns), F32)
    field = ((order, columns), F32)
    square = ((order, order), BF16)
    pair = pltpu.VMEM((order, 2 * columns), BF16)

    to_faces, *faces = call(
        load_kernel,
        [square] + [block] * 4,
        [("a", load_cases), ("v", place_column)],
        [pair, pltpu.VMEM((order, columns), F32), pltpu.SemaphoreType.DMA],
        LARGE,
    )
    received = exchange(faces)
    (to_local,) = call(onehot_kernel, [square], [("v", place_row)])
    basis_rows, basis_columns = call(
        basis_kernel,
        [((4 * modes, order), BF16), ((order, 2 * modes), BF16)],
        [("v", x) for x in (coarse_basis, group_modes, to_local, to_faces)],
        limit=LARGE,
    )
    inverse = call(split_kernel, [square] * 2, [("v", local_inverse), ("a", basis_rows)])
    received, inverse = lax.optimization_barrier((received, inverse))
    schur = [None, None]

    def schur_part(part, after):
        ins = [("v", schur_matrix), ("v", to_local), ("a", after)]
        kernel = functools.partial(columns_kernel, part)
        return call(kernel, [square], ins, limit=LARGE, flops=1 << 31)[0]

    def schur_rows(part, after):
        ins = [("v", part), ("v", to_faces), ("a", after)]
        return call(rows_kernel, [square], ins, limit=LARGE, flops=1 << 31)[0]

    def update(residual, faces, received):
        first = residual is None
        ins = [("s", numbers), ("v", basis_rows)]
        ins += ([] if first else [("v", residual)]) + [("v", x) for x in faces + received]
        return call(
            functools.partial(residual_kernel, first),
            [field, ((order, 2 * columns), BF16), ((2 * modes, columns), F32)],
            ins,
            limit=LARGE,
        )

    def precondition(step, weighted, coarse_top):
        def product():
            return call(
                product_kernel,
                [block] * 4,
                [("v", x) for x in (*inverse, to_local, to_faces, weighted)],
                [pair] * 2,
                LARGE,
                flops=1 << 30,
            )

        others = [across_sub(coarse_top, mask) for mask in (8, 24, 16)]
        if step == 0:
            others, schur[0] = lax.optimization_barrier((others, schur_part(0, coarse_top)))
        if step == 1:
            others, schur[1] = lax.optimization_barrier((others, schur_rows(schur[1], coarse_top)))
        (level,) = call(
            functools.partial(level_kernel, modes),
            [((5 * modes, columns), F32)],
            [("v", x) for x in (coarse_top, others[0], others[2], others[1])],
        )
        others = [across_sub(level, mask) for mask in (2, 6, 4)]
        others, local_part = lax.optimization_barrier((others, product()))
        (level,) = call(
            functools.partial(level_kernel, modes),
            [((17 * modes, columns), F32)],
            [("v", x) for x in (level, others[0], others[2], others[1])],
        )
        gathered = [("v", level), ("v", across_core(level))]
        (top_term,) = call(total_kernel, [((modes, columns), F32)], gathered)
        (grouped,) = call(
            group_kernel,
            [((modes, columns), F32)],
            [("s", place), ("v", group_inverse)] + gathered,
            [pltpu.VMEM((group_inverse.shape[1], 2 * columns), BF16)],
            flops=1 << 26,
        )
        others = [across_grp(top_term, mask) for mask in (1, 3, 2)]
        others, grouped = lax.optimization_barrier((others, grouped))
        other, ordered = call(
            apex_kernel,
            [((modes, columns), F32), ((4 * modes, columns), F32)],
            [("s", place), ("v", top_inverse)] + [("v", x) for x in (top_term, others[0], others[2], others[1])],
        )
        theirs = across_grp(other, 4)
        (partial,) = call(
            partial_kernel,
            [((modes, columns), F32)],
            [("s", place)] + [("v", x) for x in (top_inverse, group_modes, ordered, grouped)],
        )
        theirs, partial = lax.optimization_barrier((theirs, partial))
        ins = [basis_columns, group_modes, partial, theirs] + local_part
        return call(
            prolong_kernel,
            [block] * 4,
            [("s", numbers)] + [("v", x) for x in ins],
            limit=LARGE,
        )

    residual = direction = solved = None
    for step in range(ITERS):
        residual, weighted, coarse_top = update(residual, faces, received)
        faces = precondition(step, weighted, coarse_top)
        received = exchange(faces)
        if step == 0:
            received, schur[1] = lax.optimization_barrier((received, schur_part(1, faces[3])))
        ins = [("s", numbers)]
        ins += [("v", x) for x in schur] + ([("v", to_faces)] if step == 0 else [])
        ins += [] if step == 0 else [("v", direction), ("v", solved)]
        direction, solved, *faces = call(
            functools.partial(direction_kernel, step),
            [field, field] + [block] * 4,
            ins + [("v", x) for x in faces + received],
            [pair] * 2,
            LARGE,
            flops=1 << 30,
        )
        received = exchange(faces)
        if step == 0:
            received, schur[0] = lax.optimization_barrier((received, schur_rows(schur[0], faces[3])))
    (displacement,) = call(
        local_kernel, [field], [("v", to_local), ("v", solved)], [pair], LARGE, flops=1 << 28
    )
    (remainder,) = call(
        last_kernel,
        [field],
        [("s", numbers), ("v", to_local), ("v", residual)] + [("v", x) for x in faces + received],
        [pltpu.VMEM((order, columns), F32), pair],
        LARGE,
    )
    return displacement, remainder


def solution(mesh):
    placed = (
        P(("grp", "sub"), None),
        P(("grp", "sub"), None),
        P(("grp", "sub"), None),
        P(("grp", "sub"), None),
        P(("grp", "sub"), None),
        P(("grp", "sub"), None),
        P(),
        P(("grp", "sub"), None),
        P(),
    )
    return jax.shard_map(
        shards,
        mesh=mesh,
        in_specs=placed,
        out_specs=(P(("grp", "sub"), None), P(("grp", "sub"), None)),
        check_vma=False,
    )
```
